32 devices in a mesh: scene: 2 (over y), curve: 4 (over z), slab: 4 (over x, core).
Axes of the slice: x: 2, y: 2, z: 4, core: 2. Of those that a mesh axis runs over, the one named last changes fastest.
Arguments:
- features: bfloat16 [256, 32, 512], P(('scene', 'curve', 'slab')), parts along dimension 0, may hold values from -6 to 6
- voxel_mask: int32 [256, 512], P(('scene', 'curve', 'slab')), parts along dimension 0, may hold values 0 or 1
- weights: bfloat16 [27, 32, 32], replicated, may hold values from -0.21875 to 0.21875
- grad_out: bfloat16 [256, 32, 512], P(('scene', 'curve', 'slab')), parts along dimension 0, may hold values from -6 to 6
- send_list: int32 [32, 8, 2], P(('scene', 'curve', 'slab')), parts along dimension 0, may hold values from -1 to 7, as said below
- kernel_map: int32 [256, 27], P(('scene', 'curve', 'slab')), parts along dimension 0, may hold values from -1 to 23, as said below
Outputs:
- convolved: bfloat16 [256, 32, 512], P(('scene', 'curve', 'slab')), parts along dimension 0
- grad_features: float32 [256, 32, 512], P(('scene', 'curve', 'slab')), parts along dimension 0
- grad_weights: float32 [54, 32, 32], P('scene'), parts along dimension 0
The draws below stay inside these ranges and needn't reach their ends.
There are 2 independent parts, one for each index of `scene`. The reference program is written for one: setup_inputs(seed, part) draws one part's arguments, and reference() takes and returns one part's arrays. A program takes and returns all parts, laid end to end along the dimension named above; an argument that names none is the same for every part. Nothing has to cross between parts.
Inputs may be any that keep to these rules, and one draw needn't show every extreme that they name: send_list[q, u, k] lists, in slot k, a brick of range q (as an index within the range) that range (q + d(u)) mod 16 receives; -1 marks an empty slot. The slot with u = 7 and k = 1 is filled in every row. `kernel_map`: entry [b, j] for brick b of range r is -1 (no brick), an index i below 8 (brick r * 8 + i), or 8 + u * 2 + k, which names slot k of send_list[(r - d(u)) mod 16, u], never an empty slot. Column 13 holds the brick's own index within its range.
All inputs are finite; a program needn't handle non-finite values. No bound on the sum of `voxel_mask` on one device may be relied on, other than what follows from the above.
Results may differ from the reference program's by a relative error of at most 0.002.
Values may be sent and summed in bfloat16 or wider, within the bound.
No kernel may reach another device: no remote copies, remote signals or barrier semaphores. Data moves between devices by JAX's collectives and lax.ppermute only.
A program may use at most 64 MiB of HBM per device.

```python
import math
import jax
import jax.numpy as jnp
from jax import lax

C = 32
V = 512
BD = 8
HALO = 4
CAP = 2
PEERS = 16
BRICKS = 128


def open_slots(key):
    key = jax.random.fold_in(key, 101)
    coin_value = jax.random.randint(key, (PEERS, 2 * HALO, CAP), 0, 4)
    slot_place = jnp.arange(2 * HALO * CAP, dtype=jnp.int32).reshape(1, 2 * HALO, CAP)
    forced = slot_place == 2 * HALO * CAP - 1
    return (coin_value > 0) | forced


def draw_send_list(key, part):
    opened = open_slots(key)
    key = jax.random.fold_in(key, 3)
    picked = jax.random.randint(key, (PEERS, 2 * HALO, CAP), 0, BD)
    return jnp.where(opened, picked, -1).astype(jnp.int32)


def draw_kernel_map(key, part):
    opened = open_slots(key)
    key = jax.random.fold_in(key, 5)
    kind_key, local_key, offset_key, column_key = jax.random.split(key, 4)
    kind_value = jax.random.randint(kind_key, (BRICKS, 27), 0, 8)
    local_index = jax.random.randint(local_key, (BRICKS, 27), 0, BD)
    offset_slot = jax.random.randint(offset_key, (BRICKS, 27), 0, 2 * HALO)
    column = jax.random.randint(column_key, (BRICKS, 27), 0, CAP)
    owner_range = (jnp.arange(BRICKS, dtype=jnp.int32) // BD)[:, None]
    distance = jnp.where(offset_slot < HALO, offset_slot + 1, -(offset_slot - HALO + 1))
    source = (owner_range - distance) % PEERS
    open_ref = opened[source, offset_slot, column]
    remote = jnp.where(open_ref, BD + offset_slot * CAP + column, -1)
    entries = jnp.where(kind_value < 2, -1, jnp.where(kind_value < 5, local_index, remote))
    own_index = jnp.arange(BRICKS, dtype=jnp.int32) % BD
    column_place = jnp.arange(27, dtype=jnp.int32)[None, :]
    first_brick = (own_index == 0)[:, None] & (column_place == 0)
    entries = jnp.where(first_brick, BD + 2 * HALO * CAP - 1, entries)
    return jnp.where(column_place == 13, own_index[:, None], entries).astype(jnp.int32)


def set_ends(values, own_key, least, high):
    longest = values.shape.index(max(values.shape))
    spots = []
    for shift in (0, 1):
        where = [jax.random.randint(jax.random.fold_in(own_key, axis), (), 0, length) for axis, length in enumerate(values.shape)]
        where[longest] = (where[longest] + shift) % values.shape[longest]
        spots.append(tuple(where))
    return values.at[spots[0]].set(least).at[spots[1]].set(high)


def steps_of(key, dims, cuts, smallest, top_value):
    factor_of, own = 1.0, jax.random.fold_in(key, 6)
    for axis_at, parts in cuts:
        draws = jnp.exp(jax.random.uniform(jax.random.fold_in(own, axis_at), (parts,), jnp.float32, smallest / len(cuts), top_value / len(cuts)))
        factor_of = factor_of * jnp.repeat(draws, dims[axis_at] // parts).reshape([-1 if axis == axis_at else 1 for axis in range(len(dims))])
    return factor_of


def bell_draw(stream_key, dims, scale, most, shards=(), kind=jnp.bfloat16):
    drawn = scale * jax.random.normal(stream_key, dims, jnp.float32)
    if shards:
        drawn = drawn * steps_of(stream_key, dims, shards, -0.22, 0.18)
    return jnp.clip(drawn, -most, most).astype(kind)


def setup_inputs(seed: int = 0, part: int = 0) -> dict:
    key_list = jax.random.split(jax.random.key(seed), 7)
    part_splits = jax.random.split(jax.random.fold_in(key_list[6], part), 7)
    return {
        "features": bell_draw(part_splits[0], (BRICKS, C, V), 1.0, 6.0, ((0, 16),)),
        "voxel_mask": set_ends((jax.random.randint(part_splits[1], (BRICKS, V), 0, 2) < 1).astype(jnp.int32), jax.random.fold_in(part_splits[1], 1), 0, 1),
        "weights": bell_draw(key_list[2], (27, C, C), (27 * C) ** -0.5, 0.21875),
        "grad_out": bell_draw(part_splits[3], (BRICKS, C, V), 1.0, 6.0, ((0, 16),)),
        "send_list": draw_send_list(jax.random.fold_in(jax.random.fold_in(key_list[6], part), 71), part),
        "kernel_map": draw_kernel_map(jax.random.fold_in(jax.random.fold_in(key_list[6], part), 71), part),
    }


def along(stacked, position, stride):
    place = jnp.arange(stacked.shape[-1], dtype=jnp.int32)
    coordinate = place // stride % 8
    below_brick = lax.index_in_dim(stacked, 0, position, keepdims=False)
    centre = lax.index_in_dim(stacked, 1, position, keepdims=False)
    above_brick = lax.index_in_dim(stacked, 2, position, keepdims=False)
    downward = jnp.where(coordinate == 0, jnp.roll(below_brick, -7 * stride, -1), jnp.roll(centre, stride, -1))
    upward = jnp.where(coordinate == 7, jnp.roll(above_brick, 7 * stride, -1), jnp.roll(centre, -stride, -1))
    return jnp.stack([downward, centre, upward], axis=position)

def shifted_taps(nearby):
    return along(along(along(nearby, 2, 1), 1, 8), 0, 64)

def global_neighbours(send_list, kernel_map):
    brick_index = jnp.arange(BRICKS, dtype=jnp.int32)
    owner_range = (brick_index // BD)[:, None]
    local_id = owner_range * BD + kernel_map
    slot_index = jnp.maximum(kernel_map - BD, 0)
    offset_slot = slot_index // CAP
    column = slot_index % CAP
    distance = jnp.where(offset_slot < HALO, offset_slot + 1, -(offset_slot - HALO + 1))
    source = (owner_range - distance) % PEERS
    sent_brick = send_list[source, offset_slot, column]
    remote = jnp.where(sent_brick >= 0, source * BD + sent_brick, -1)
    picked = jnp.where(kernel_map < BD, local_id, remote)
    return jnp.where(kernel_map < 0, -1, picked).astype(jnp.int32)

def reference(features, voxel_mask, weights, grad_out, send_list, kernel_map):
    active = voxel_mask.astype(jnp.float32)[:, None, :]
    masked = features.astype(jnp.float32) * active
    masked_grad = grad_out.astype(jnp.float32) * active
    weight_full = weights.astype(jnp.float32)
    global_ids = global_neighbours(send_list, kernel_map)
    block_len = math.gcd(BRICKS, 64)
    blank_field = jnp.zeros((3, 3, 3, block_len, C, V), jnp.float32)

    def advance(running, first_row):
        grad_masked, grad_weight = running
        neighbours = lax.dynamic_slice_in_dim(global_ids, first_row, block_len, 0)
        present_mask = (neighbours >= 0).astype(jnp.float32)[:, :, None, None]
        nearby = jnp.take(masked, jnp.maximum(neighbours, 0).reshape(-1), axis=0)
        nearby = nearby.reshape(block_len, 27, C, V) * present_mask
        nearby = jnp.moveaxis(nearby, 1, 0).reshape(3, 3, 3, block_len, C, V)
        shifted = shifted_taps(nearby).reshape(27, block_len, C, V)
        partial_out = jnp.einsum('tbiv,toi->bov', shifted, weight_full, precision=lax.Precision.HIGHEST)
        cotangent_block = lax.dynamic_slice_in_dim(masked_grad, first_row, block_len, 0)
        grad_weight = grad_weight + jnp.einsum('bov,tbiv->toi', cotangent_block, shifted, precision=lax.Precision.HIGHEST)
        pulled = jnp.einsum('bov,toi->tbiv', cotangent_block, weight_full, precision=lax.Precision.HIGHEST)
        unshift = jax.vjp(shifted_taps, blank_field)[1]
        spread = unshift(pulled.reshape(3, 3, 3, block_len, C, V))[0]
        spread = jnp.moveaxis(spread.reshape(27, block_len, C, V), 0, 1) * present_mask
        grad_masked = grad_masked.at[jnp.maximum(neighbours, 0).reshape(-1)].add(spread.reshape(-1, C, V))
        return ((grad_masked, grad_weight), partial_out)
    starts = jnp.arange(0, BRICKS, block_len, dtype=jnp.int32)
    initial = (jnp.zeros((BRICKS, C, V), jnp.float32), jnp.zeros((27, C, C), jnp.float32))
    (grad_masked, grad_weight), outputs = lax.scan(advance, initial, starts)
    convolved = (outputs.reshape(BRICKS, C, V) * active).astype(jnp.bfloat16)
    grad_features = grad_masked * active
    grad_weights = grad_weight / math.sqrt(BRICKS * V)
    return (convolved, grad_features, grad_weights)
```

```python
import functools
import math

import jax
import jax.numpy as jnp
from jax import lax
from jax.experimental import pallas as pl
from jax.experimental.pallas import tpu as pltpu
from jax.sharding import PartitionSpec as P

F32 = jnp.float32
BF16 = jnp.bfloat16
RANGE_AXES = ("curve", "slab")
VMEM = pl.BlockSpec(memory_space=pltpu.VMEM)
SMEM = pl.BlockSpec(memory_space=pltpu.SMEM)
NT = (((1,), (1,)), ((), ()))
NN = (((1,), (0,)), ((), ()))
TN = (((0,), (0,)), ((), ()))

BLOCK = 192
DUMMY = 24


def iota(shape, axis):
    return lax.broadcasted_iota(jnp.int32, shape, axis)


def dot(a, b, dims):
    return lax.dot_general(a, b, dims, preferred_element_type=F32)


def col(jx, jy, jz):
    return 9 * (jx + 1) + 3 * (jy + 1) + (jz + 1)


def voxel_order():
    row = iota((512, 512), 0)
    return jnp.where(iota((512, 512), 1) == ((row & 63) << 3) + (row >> 6), 1.0, 0.0).astype(BF16)


def swap_blocks(parts):
    lane = iota((64, 128), 1)
    half = [[p[:, :128], p[:, 128:]] for p in parts]
    now = [[half[(h << 2) | (i & 3)][i >> 2] for h in range(2)] for i in range(8)]
    for bit, shift in ((1, 64), (0, 32)):
        low = (lane & shift) == 0
        for i in range(8):
            if i >> bit & 1:
                continue
            j = i | (1 << bit)
            for h in range(2):
                p, q = now[i][h], now[j][h]
                now[i][h] = jnp.where(low, p, pltpu.roll(q, shift, 1))
                now[j][h] = jnp.where(low, pltpu.roll(p, 128 - shift, 1), q)
    return [jnp.concatenate(n, axis=1) for n in now]


def to_rows(values, order):
    swapped = dot(order, values, NT)
    return swap_blocks([swapped[64 * z : 64 * z + 64] for z in range(8)])


def masked_values(values, mask):
    return (values.astype(F32) * mask.astype(F32)[:, None, :]).astype(BF16).reshape(256, 512)


def parity():
    return (lax.axis_index("curve") * lax.axis_size("slab") + lax.axis_index("slab")) & 1


def entry_of(kmap, b, j, flip):
    e = kmap[b, j]
    far = ((e - 8) ^ flip) + 8
    return jnp.where(e < 0, DUMMY, jnp.where(e < 8, e, far))


def pack_kernel(feat, mask, send, first, own, center, xf, yf, zf):
    bricks = to_rows(masked_values(feat[...], mask[...]), voxel_order())
    lane = iota((64, 128), 1)
    for b in range(8):
        c = bricks[b]
        for h in range(2):
            center[b, h] = c[:, 128 * h : 128 * h + 128]
        xf[b, 0:8] = c[0:8]
        xf[b, 8:16] = c[56:64]
        for h in range(2):
            s = slice(128 * h, 128 * h + 128)
            yf[b, 0:8, s] = center[b, h, pl.ds(0, 8, 8), :]
            yf[b, 8:16, s] = center[b, h, pl.ds(7, 8, 8), :]
        lo, hi = c[:, :128], c[:, 128:]
        even = jnp.where(lane < 64, pltpu.roll(hi, 32, 1), pltpu.roll(hi, 96, 1))
        odd = jnp.where(lane < 64, pltpu.roll(lo, 32, 1), pltpu.roll(lo, 96, 1))
        zf[b] = jnp.where((lane & 32) == 0, even, odd)
    flip = parity() * 4

    def put(out, at, u):
        pick = [jnp.maximum(send[0, u, k], 0) for k in range(2)]
        for k in range(2):
            xy = jnp.concatenate([xf[pick[k]], yf[pick[k]]], axis=0).astype(BF16)
            out[at, 64 * k : 64 * k + 32] = xy[:, :128]
            out[at, 64 * k + 32 : 64 * k + 64] = xy[:, 128:]
        out[at, 128:192] = jnp.where(lane < 64, zf[pick[0]], zf[pick[1]]).astype(BF16)

    for n in range(4):
        put(first, n, (4 + n) ^ flip)
    put(first, 4, flip)
    for n in range(3):
        put(own, n, (1 + n) ^ flip)


def sublane_masks(rows):
    y = iota((rows, 8, 128), 1)
    return y == 0, y == 7


def back_kernel(cot, mask, weights, kmap, wide, stack, stack_t, center, xg, yg, zg, first, own, gp, xa, ya, za):
    flip = parity() * 8
    bricks = to_rows(masked_values(cot[...], mask[...]), voxel_order())
    for b in range(8):
        c = bricks[b]
        for d in range(3):
            before, after = jnp.zeros((8 * d, 256), F32), jnp.zeros((16 - 8 * d, 256), F32)
            pieces = [p for p in (before, c, after) if p.shape[0]]
            stack[80 * b : 80 * b + 80, 256 * d : 256 * d + 256] = jnp.concatenate(pieces, axis=0).astype(BF16)
    for d in range(3):
        stack_t[256 * d : 256 * d + 256] = stack[:, 256 * d : 256 * d + 256].T

    tile = jnp.where((iota((32, 256), 1) & 31) == iota((32, 256), 0), 1.0, 0.0).astype(BF16)
    tiled = dot(weights[...].reshape(864, 32), tile, NN)
    block = iota((32, 256), 1) >> 5

    def tap(dx, dy, dz):
        t = col(dx - 1, dy - 1, dz - 1)
        return tiled[32 * t : 32 * t + 32]

    for dx in range(3):
        for z in range(8):
            rows = slice(256 * dx + 32 * z, 256 * dx + 32 * z + 32)
            for dy in range(3):
                w = jnp.zeros((32, 256), F32)
                for dz in range(3):
                    if 0 <= z + dz - 1 <= 7:
                        w = jnp.where(block == z + dz - 1, tap(dx, dy, dz), w)
                wide[rows, 256 * dy : 256 * dy + 256] = w.astype(BF16)
            w = jnp.zeros((32, 256), F32)
            if z in (0, 7):
                for dy in range(3):
                    w = jnp.where(block == 2 * dy + (z == 7), tap(dx, dy, 0 if z == 0 else 2), w)
            wide[rows, 768:1024] = w.astype(BF16)

    for n in range(4):
        s = slice(256 * n, 256 * n + 256)
        g = dot(stack[...], wide[:, s], NN)
        gp[2 * n] = g[:, :128]
        gp[2 * n + 1] = g[:, 128:]

    xa[...] = jnp.zeros_like(xa)
    ya[...] = jnp.zeros_like(ya)
    za[...] = jnp.zeros_like(za)
    low3 = iota((10, 8, 128), 2) < 32
    lane_low = iota((8, 128), 1) < 32
    y2 = iota((8, 128), 0)

    def brick(b, carry):
        base = pl.multiple_of(80 * b, 80)
        e = lambda *j: entry_of(kmap, b, col(*j), flip)
        y0, y7 = sublane_masks(10)
        for h in range(2):
            s = slice(128 * h, 128 * h + 128)

            def part(n):
                return gp[2 * n + h, pl.ds(base, 80)].reshape(10, 8, 128)

            below, above = part(0), part(2)
            r = (
                part(1)
                + jnp.where(y7, 0.0, pltpu.roll(below, 7, 1))
                + jnp.where(y0, 0.0, pltpu.roll(above, 1, 1))
            )
            center[b, h] = r[1:9].reshape(64, 128)
            xa[e(-1, 0, 0), 8:16, s] += r[0]
            xa[e(1, 0, 0), 0:8, s] += r[9]
            ya[e(0, -1, 0), 8:16, s] += gp[h, pl.ds(base + 8, 8, 8), :]
            ya[e(0, 1, 0), 0:8, s] += gp[4 + h, pl.ds(base + 15, 8, 8), :]
            xa[e(-1, -1, 0), 15:16, s] += below[0, 0:1]
            xa[e(1, -1, 0), 7:8, s] += below[9, 0:1]
            xa[e(-1, 1, 0), 8:9, s] += above[0, 7:8]
            xa[e(1, 1, 0), 0:1, s] += above[9, 7:8]
        a = gp[6, pl.ds(base, 80)].reshape(10, 8, 128)
        below = pltpu.roll(a, 7, 1)
        above = pltpu.roll(gp[7, pl.ds(base, 80)].reshape(10, 8, 128), 1, 1)
        r = pltpu.roll(a, 64, 2) + jnp.where(y7, 0.0, below) + jnp.where(y0, 0.0, above)
        below = jnp.where(y7, below, 0.0)
        above = jnp.where(y0, above, 0.0)
        for jy, v in ((0, r), (-1, below), (1, above)):
            for jz in (-1, 1):
                w = jnp.where(low3 if jz < 0 else ~low3, v, 0.0)
                za[e(0, jy, jz)] += w[1:9].reshape(64, 128)
                za[e(-1, jy, jz), 56:64] += w[0]
                za[e(1, jy, jz), 0:8] += w[9]
        return carry

    lax.fori_loop(0, 8, brick, 0)
    for i in range(8):
        xg[i] = xa[i]
        yg[i] = ya[i]
        zg[i] = za[i]

    lane = iota((64, 128), 1)

    def put(out, at, n):
        entry = 8 + 2 * (n ^ 4)
        for k in range(2):
            xy = jnp.concatenate([xa[entry + k], ya[entry + k]], axis=0).astype(BF16)
            out[at, 64 * k : 64 * k + 32] = xy[:, :128]
            out[at, 64 * k + 32 : 64 * k + 64] = xy[:, 128:]
        out[at, 128:192] = jnp.where(lane < 64, za[entry], pltpu.roll(za[entry + 1], 64, 1)).astype(BF16)

    for n in range(4):
        put(first, n, 4 + n)
    put(first, 4, 0)
    for n in range(3):
        put(own, n, 1 + n)


def received(first, near, far, last):
    return [(near, 2), (near, 0), (far, 1), (far, 0), (first, 4), (last, 1), (last, 0), (last, 2)]


def conv_kernel(
    center, xf, yf, zf, kmap, mask, wide, stack_t, first, near, far, last, conv, grad_w, xt, yt, zt, taps
):
    flip = parity() * 8
    for i in range(8):
        xt[i] = xf[i]
        yt[i] = yf[i]
        zt[i] = zf[i]
    xt[DUMMY] = jnp.zeros((16, 256), F32)
    yt[DUMMY] = jnp.zeros((16, 256), F32)
    zt[DUMMY] = jnp.zeros((64, 128), F32)
    lane = iota((64, 128), 1)
    for n, (ref, at) in enumerate(received(first, near, far, last)):
        for k in range(2):
            entry = 8 + 2 * n + k
            for h in range(2):
                xy = ref[at, 64 * k + 32 * h : 64 * k + 32 * h + 32].astype(F32)
                xt[entry, :, 128 * h : 128 * h + 128] = xy[:16]
                yt[entry, :, 128 * h : 128 * h + 128] = xy[16:]
        z = ref[at, 128:192].astype(F32)
        turned = pltpu.roll(z, 64, 1)
        zt[8 + 2 * n] = jnp.where(lane < 64, z, turned)
        zt[9 + 2 * n] = jnp.where(lane < 64, turned, z)

    low3 = (iota((8, 8, 128), 2) & 32) == 0
    low2 = (iota((8, 128), 1) & 32) == 0
    left3 = iota((10, 8, 128), 2) < 64

    def brick(b, carry):
        base = pl.multiple_of(80 * b, 16)
        e = lambda *j: entry_of(kmap, b, col(*j), flip)
        y0, y7 = sublane_masks(10)
        for h in range(2):
            s = slice(128 * h, 128 * h + 128)
            r = jnp.concatenate(
                [
                    xt[e(-1, 0, 0), 8:16, s].reshape(1, 8, 128),
                    center[b, h].reshape(8, 8, 128),
                    xt[e(1, 0, 0), 0:8, s].reshape(1, 8, 128),
                ],
                axis=0,
            )

            def edge(jy, y_rows, x_row):
                first_row = xt[e(-1, jy, 0), 8 + x_row : 9 + x_row, s]
                last_row = xt[e(1, jy, 0), x_row : x_row + 1, s]
                entry = e(0, jy, 0)
                middle = [yt[entry, y_rows + x : y_rows + x + 1, s] for x in range(8)]
                rows = [first_row] + middle + [last_row]
                return jnp.stack([jnp.broadcast_to(row, (8, 128)) for row in rows], axis=0)

            below = jnp.where(y0, edge(-1, 8, 7), pltpu.roll(r, 1, 1))
            above = jnp.where(y7, edge(1, 0, 0), pltpu.roll(r, 7, 1))
            for n, v in enumerate((below, r, above)):
                taps[pl.ds(base, 80), 256 * n + 128 * h : 256 * n + 128 * h + 128] = v.reshape(80, 128).astype(BF16)

        def halo(jy):
            lo, hi = e(0, jy, -1), e(0, jy, 1)
            middle = jnp.where(low3, zt[lo].reshape(8, 8, 128), zt[hi].reshape(8, 8, 128))
            start = jnp.where(low2, zt[e(-1, jy, -1), 56:64], zt[e(-1, jy, 1), 56:64])
            end = jnp.where(low2, zt[e(1, jy, -1), 0:8], zt[e(1, jy, 1), 0:8])
            return jnp.concatenate([start[None], middle, end[None]], axis=0)

        r = halo(0)
        below = pltpu.roll(jnp.where(y7, halo(-1), r), 1, 1)
        above = pltpu.roll(jnp.where(y0, halo(1), r), 7, 1)
        taps[pl.ds(base, 80), 768:896] = jnp.where(left3, below, r).reshape(80, 128).astype(BF16)
        taps[pl.ds(base, 80), 896:1024] = jnp.where(left3, above, 0.0).reshape(80, 128).astype(BF16)
        return carry

    lax.fori_loop(0, 8, brick, 0)

    tap_lane = iota((32, 128), 1)
    pieces = []
    for dx in range(3):
        full = dot(stack_t[256 * dx : 256 * dx + 256], taps[...], NN)
        for dy in range(3):
            total = jnp.zeros((32, 128), F32)
            for z in range(8):
                rows = full[32 * z : 32 * z + 32]
                lo = rows[:, 256 * dy : 256 * dy + 128]
                hi = rows[:, 256 * dy + 128 : 256 * dy + 256]
                edge_tile = rows[:, 768 + 128 * (dy // 2) : 896 + 128 * (dy // 2)]
                at = 64 * (dy % 2)
                if z == 0:
                    v = jnp.where(tap_lane < 32, pltpu.roll(edge_tile, (128 - at) % 128, 1), pltpu.roll(lo, 32, 1))
                elif z == 7:
                    v = jnp.where(tap_lane < 64, pltpu.roll(hi, 64, 1), pltpu.roll(edge_tile, (32 - at) % 128, 1))
                else:
                    q = 32 * (z - 1)
                    left, right = (lo, lo) if q < 64 else (lo, hi) if q < 128 else (hi, hi)
                    if left is right:
                        v = pltpu.roll(left, (256 - q) % 128, 1) if q % 128 else left
                    else:
                        v = jnp.where(
                            tap_lane < 128 - q,
                            pltpu.roll(left, 128 - q, 1),
                            pltpu.roll(right, 128 - q, 1),
                        )
                total = total + v
            pieces.append(jnp.where(tap_lane < 96, total, 0.0))
    tiles = [jnp.zeros((32, 128), F32) for _ in range(7)]
    for n, piece in enumerate(pieces):
        start = 96 * n
        at, tile = start % 128, start // 128
        turned = pltpu.roll(piece, at, 1) if at else piece
        if at + 96 <= 128:
            tiles[tile] = tiles[tile] + turned
        else:
            tiles[tile] = tiles[tile] + jnp.where(tap_lane >= at, turned, 0.0)
            tiles[tile + 1] = tiles[tile + 1] + jnp.where(tap_lane < at, turned, 0.0)
    for n in range(7):
        grad_w[:, 128 * n : 128 * n + 128] = tiles[n]

    pre = jnp.zeros((8, 8, 8, 256), F32)
    for dx in range(3):
        u = dot(taps[...], wide[256 * dx : 256 * dx + 256], NT).reshape(8, 10, 8, 256)
        pre = pre + u[:, dx : dx + 8]
    by_z = swap_blocks([pre[b].reshape(64, 256) for b in range(8)])
    stacked = jnp.concatenate([v.astype(BF16) for v in by_z], axis=0)
    out = dot(stacked.T, voxel_order(), NN).reshape(8, 32, 512)
    conv[...] = (out * mask[...].astype(F32)[:, None, :]).astype(BF16)


def fold_kernel(center, xg, yg, zg, mask, send, first, near, far, last, out, xa, ya, za):
    flip = parity() * 4
    xa[...] = xg[...]
    ya[...] = yg[...]
    za[...] = zg[...]
    for n, (ref, at) in enumerate(received(first, near, far, last)):
        u = n ^ 4 ^ flip
        z = ref[at, 128:192].astype(F32)
        for k in range(2):
            i = jnp.maximum(send[0, u, k], 0)
            for h in range(2):
                xy = ref[at, 64 * k + 32 * h : 64 * k + 32 * h + 32].astype(F32)
                xa[i, :, 128 * h : 128 * h + 128] += xy[:16]
                ya[i, :, 128 * h : 128 * h + 128] += xy[16:]
            za[i] += pltpu.roll(z, 64, 1) if k else z
    y0, y7 = sublane_masks(8)
    lane = iota((64, 128), 1)
    bricks = []
    for b in range(8):
        turned = pltpu.roll(za[b], 96, 1)
        halves = []
        for h in range(2):
            s = slice(128 * h, 128 * h + 128)
            c = center[b, h] + jnp.where(lane >= 96 if h else lane < 32, turned, 0.0)
            c = c.reshape(8, 8, 128)
            c = jnp.concatenate([c[0:1] + xa[b, 0:8, s][None], c[1:7], c[7:8] + xa[b, 8:16, s][None]], axis=0)
            low = jnp.stack([jnp.broadcast_to(ya[b, x : x + 1, s], (8, 128)) for x in range(8)], axis=0)
            high = jnp.stack([jnp.broadcast_to(ya[b, 8 + x : 9 + x, s], (8, 128)) for x in range(8)], axis=0)
            c = c + jnp.where(y0, low, 0.0) + jnp.where(y7, high, 0.0)
            halves.append(c.reshape(64, 128))
        bricks.append(jnp.concatenate(halves, axis=1))
    rows = jnp.concatenate(swap_blocks(bricks), axis=0).T
    coarse = rows.astype(BF16)
    fine = (rows - coarse.astype(F32)).astype(BF16)
    order = voxel_order()
    full = dot(coarse, order, NN) + dot(fine, order, NN)
    out[...] = full.reshape(8, 32, 512) * mask[...].astype(F32)[:, None, :]


def spread_kernel(scale, wide, out):
    for t in range(27):
        at, tile = 32 * t % 128, 32 * t // 128
        v = wide[:, 128 * tile : 128 * tile + 128]
        v = pltpu.roll(v, 128 - at, 1) if at else v
        out[t] = v[:, :32] * scale


def call(kernel, outs, scratch, ins, flops=0, size=0):
    return pl.pallas_call(
        kernel,
        out_shape=[jax.ShapeDtypeStruct(s, d) for s, d in outs],
        in_specs=ins,
        out_specs=[VMEM] * len(outs),
        scratch_shapes=[pltpu.VMEM(s, d) for s, d in scratch],
        compiler_params=pltpu.CompilerParams(vmem_limit_bytes=40 * 1024 * 1024),
        cost_estimate=pl.CostEstimate(flops=flops, bytes_accessed=size, transcendentals=0),
    )


def permute(value, target):
    count = lax.axis_size(RANGE_AXES)
    return lax.ppermute(value, RANGE_AXES, [(r, target(r, count)) for r in range(count)])


def swap(value, bit=1):
    return permute(value, lambda r, count: r ^ bit)


def onward(value, pairs):
    return permute(value, lambda r, count: (r + (-2 * pairs if r & 1 else 2 * pairs)) % count)


def exchange(first, own):
    first = swap(first)
    near = onward(jnp.concatenate([own[0:2], first[0:2]], axis=0), 1)
    far = onward(jnp.concatenate([own[2:3], first[2:4]], axis=0), 2)
    last = swap(jnp.concatenate([near[1:2], near[3:4], far[2:3]], axis=0))
    return first, near, far, last


def total_over_ranges(value):
    bit = 1
    while bit < lax.axis_size(RANGE_AXES):
        value = value + swap(value, bit)
        bit *= 2
    return value


def body(features, voxel_mask, weights, grad_out, send_list, kernel_map):
    block = lambda n: ((n, BLOCK, 128), BF16)
    faces = [((8, 16, 256), F32), ((8, 16, 256), F32), ((8, 64, 128), F32)]
    center_shape = ((8, 2, 64, 128), F32)

    first, own, center, xf, yf, zf = call(
        pack_kernel, [block(5), block(3), center_shape] + faces, [], [VMEM, VMEM, SMEM], 2 * 512 * 512 * 256, 1 << 21
    )(features, voxel_mask, send_list)
    got = exchange(first, own)

    accumulators = [((25, 16, 256), F32), ((25, 16, 256), F32), ((25, 64, 128), F32)]
    wide, stack, stack_t, grad_center, xg, yg, zg, grad_first, grad_own = call(
        back_kernel,
        [((768, 1024), BF16), ((640, 768), BF16), ((768, 640), BF16), center_shape] + faces + [block(5), block(3)],
        [((8, 640, 128), F32)] + accumulators,
        [VMEM, VMEM, VMEM, SMEM],
        2 * 640 * 768 * 1024,
        8 << 20,
    )(grad_out, voxel_mask, weights, kernel_map)
    grad_got = exchange(grad_first, grad_own)

    conv, grad_w = call(
        conv_kernel,
        [((8, 32, 512), BF16), ((32, 896), F32)],
        accumulators + [((640, 1024), BF16)],
        [VMEM] * 4 + [SMEM] + [VMEM] * 7,
        4 * 640 * 768 * 1024,
        8 << 20,
    )(center, xf, yf, zf, kernel_map, voxel_mask, wide, stack_t, *got)
    grad_w = total_over_ranges(grad_w)

    (grad_features,) = call(
        fold_kernel,
        [((8, 32, 512), F32)],
        faces,
        [VMEM] * 5 + [SMEM] + [VMEM] * 4,
        2 * 512 * 512 * 512,
        4 << 20,
    )(grad_center, xg, yg, zg, voxel_mask, send_list, *grad_got)

    brick_count, _, voxels = features.shape
    scale = 1.0 / math.sqrt(brick_count * lax.axis_size(RANGE_AXES) * voxels)
    (grad_weights,) = call(functools.partial(spread_kernel, scale), [((27, 32, 32), F32)], [], [VMEM])(grad_w)
    return conv, grad_features, grad_weights


def solution(mesh):
    bricks = ("scene", "curve", "slab")
    return jax.shard_map(
        body,
        mesh=mesh,
        in_specs=(
            P(bricks, None, None),
            P(bricks, None),
            P(),
            P(bricks, None, None),
            P(bricks, None, None),
            P(bricks, None),
        ),
        out_specs=(
            P(bricks, None, None),
            P(bricks, None, None),
            P("scene", None, None),
        ),
        check_vma=False,
    )
```

```python
import functools
import math

import jax
import jax.numpy as jnp
from jax import lax
from jax.experimental import pallas as pl
from jax.experimental.pallas import tpu as pltpu
from jax.sharding import PartitionSpec as P

F32 = jnp.float32
BF16 = jnp.bfloat16
RANGE_AXES = ("curve", "slab")
VMEM = pl.BlockSpec(memory_space=pltpu.VMEM)
HBM = pl.BlockSpec(memory_space=pltpu.HBM)
NT = (((1,), (1,)), ((), ()))
NN = (((1,), (0,)), ((), ()))
TN = (((0,), (0,)), ((), ()))

BLOCK = 192
DUMMY = 24


def iota(shape, axis):
    return lax.broadcasted_iota(jnp.int32, shape, axis)


def dot(a, b, dims):
    return lax.dot_general(a, b, dims, preferred_element_type=F32)


def col(jx, jy, jz):
    return 9 * (jx + 1) + 3 * (jy + 1) + (jz + 1)


def voxel_order():
    row = iota((512, 512), 0)
    return jnp.where(iota((512, 512), 1) == ((row & 63) << 3) + (row >> 6), 1.0, 0.0).astype(BF16)


def swap_blocks(parts):
    lane = iota((64, 128), 1)
    half = [[p[:, :128], p[:, 128:]] for p in parts]
    now = [[half[(h << 2) | (i & 3)][i >> 2] for h in range(2)] for i in range(8)]
    for bit, shift in ((1, 64), (0, 32)):
        low = (lane & shift) == 0
        for i in range(8):
            if i >> bit & 1:
                continue
            j = i | (1 << bit)
            for h in range(2):
                p, q = now[i][h], now[j][h]
                now[i][h] = jnp.where(low, p, pltpu.roll(q, shift, 1))
                now[j][h] = jnp.where(low, pltpu.roll(p, 128 - shift, 1), q)
    return [jnp.concatenate(n, axis=1) for n in now]


def to_rows(values, order):
    swapped = dot(order, values, NT)
    return swap_blocks([swapped[64 * z : 64 * z + 64] for z in range(8)])


def masked_values(values, mask):
    return (values.astype(F32) * mask.astype(F32)[:, None, :]).astype(BF16).reshape(256, 512)


def parity():
    return (lax.axis_index("curve") * lax.axis_size("slab") + lax.axis_index("slab")) & 1


def fetch(*pairs):
    copies = [pltpu.make_async_copy(src, dst, sem) for src, dst, sem in pairs]
    for c in copies:
        c.start()
    return copies


def pack_kernel(feat_hbm, mask_hbm, send_hbm, first, own_near, own_far, center, xf, yf, zf, feat, mask, send, sems):
    copies = fetch((feat_hbm, feat, sems.at[0]), (mask_hbm, mask, sems.at[1]), (send_hbm, send, sems.at[2]))
    order = voxel_order()
    for c in copies:
        c.wait()
    bricks = to_rows(masked_values(feat[...], mask[...]), order)
    lane = iota((64, 128), 1)
    for b in range(8):
        c = bricks[b]
        for h in range(2):
            center[b, h] = c[:, 128 * h : 128 * h + 128]
        xf[b, 0:8] = c[0:8]
        xf[b, 8:16] = c[56:64]
        for h in range(2):
            s = slice(128 * h, 128 * h + 128)
            yf[b, 0:8, s] = center[b, h, pl.ds(0, 8, 8), :]
            yf[b, 8:16, s] = center[b, h, pl.ds(7, 8, 8), :]
        lo, hi = c[:, :128], c[:, 128:]
        even = jnp.where(lane < 64, pltpu.roll(hi, 32, 1), pltpu.roll(hi, 96, 1))
        odd = jnp.where(lane < 64, pltpu.roll(lo, 32, 1), pltpu.roll(lo, 96, 1))
        zf[b] = jnp.where((lane & 32) == 0, even, odd)
    flip = parity() * 4

    def put(out, at, u):
        pick = [jnp.maximum(send[k, u], 0) for k in range(2)]
        for k in range(2):
            xy = jnp.concatenate([xf[pick[k]], yf[pick[k]]], axis=0).astype(BF16)
            out[at, 64 * k : 64 * k + 32] = xy[:, :128]
            out[at, 64 * k + 32 : 64 * k + 64] = xy[:, 128:]
        out[at, 128:192] = jnp.where(lane < 64, zf[pick[0]], zf[pick[1]]).astype(BF16)

    for n in range(4):
        put(first, n, (4 + n) ^ flip)
    put(first, 4, flip)
    for n in range(2):
        put(own_near, n, (1 + n) ^ flip)
    put(own_far, 0, 3 ^ flip)


def sublane_masks(rows):
    y = iota((rows, 8, 128), 1)
    return y == 0, y == 7


def back_kernel(
    cot_hbm, mask_hbm, weights_hbm, kmap_hbm,
    wide, stack_t, center, xg, yg, zg, entries, first, own_near, own_far,
    cot, mask, weights, kmap, stack, gp, xa, ya, za, table, sems,
):
    copies = fetch(
        (weights_hbm, weights, sems.at[0]),
        (kmap_hbm, kmap, sems.at[1]),
        (cot_hbm, cot, sems.at[2]),
        (mask_hbm, mask, sems.at[3]),
    )
    order = voxel_order()
    copies[0].wait()
    tile = jnp.where((iota((32, 256), 1) & 31) == iota((32, 256), 0), 1.0, 0.0).astype(BF16)
    tiled = dot(weights[...].reshape(864, 32), tile, NN)
    block = iota((32, 256), 1) >> 5

    def tap(dx, dy, dz):
        t = col(dx - 1, dy - 1, dz - 1)
        return tiled[32 * t : 32 * t + 32]

    for dx in range(3):
        for z in range(8):
            rows = slice(256 * dx + 32 * z, 256 * dx + 32 * z + 32)
            for dy in range(3):
                w = jnp.zeros((32, 256), F32)
                for dz in range(3):
                    if 0 <= z + dz - 1 <= 7:
                        w = jnp.where(block == z + dz - 1, tap(dx, dy, dz), w)
                wide[rows, 256 * dy : 256 * dy + 256] = w.astype(BF16)
            w = jnp.zeros((32, 256), F32)
            if z in (0, 7):
                for dy in range(3):
                    w = jnp.where(block == 2 * dy + (z == 7), tap(dx, dy, 0 if z == 0 else 2), w)
            wide[rows, 768:1024] = w.astype(BF16)

    copies[1].wait()
    e = kmap[...]
    entries[...] = jnp.where(e < 0, DUMMY, jnp.where(e < 8, e, ((e - 8) ^ (parity() * 8)) + 8))
    to_table = fetch((entries, table, sems.at[1]))[0]

    copies[2].wait()
    copies[3].wait()
    bricks = to_rows(masked_values(cot[...], mask[...]), order)
    for b in range(8):
        c = bricks[b]
        for d in range(3):
            before, after = jnp.zeros((8 * d, 256), F32), jnp.zeros((16 - 8 * d, 256), F32)
            pieces = [p for p in (before, c, after) if p.shape[0]]
            stack[80 * b : 80 * b + 80, 256 * d : 256 * d + 256] = jnp.concatenate(pieces, axis=0).astype(BF16)
    for d in range(3):
        stack_t[256 * d : 256 * d + 256] = stack[:, 256 * d : 256 * d + 256].T

    for n in range(4):
        s = slice(256 * n, 256 * n + 256)
        g = dot(stack[...], wide[:, s], NN)
        gp[2 * n] = g[:, :128]
        gp[2 * n + 1] = g[:, 128:]

    xa[...] = jnp.zeros_like(xa)
    ya[...] = jnp.zeros_like(ya)
    za[...] = jnp.zeros_like(za)
    to_table.wait()
    low3 = iota((10, 8, 128), 2) < 32

    def brick(b, carry):
        base = pl.multiple_of(80 * b, 80)
        e = lambda *j: table[b, col(*j)]
        y0, y7 = sublane_masks(10)
        for h in range(2):
            s = slice(128 * h, 128 * h + 128)

            def part(n):
                return gp[2 * n + h, pl.ds(base, 80)].reshape(10, 8, 128)

            below, above = part(0), part(2)
            r = (
                part(1)
                + jnp.where(y7, 0.0, pltpu.roll(below, 7, 1))
                + jnp.where(y0, 0.0, pltpu.roll(above, 1, 1))
            )
            center[b, h] = r[1:9].reshape(64, 128)
            xa[e(-1, 0, 0), 8:16, s] += r[0]
            xa[e(1, 0, 0), 0:8, s] += r[9]
            ya[e(0, -1, 0), 8:16, s] += gp[h, pl.ds(base + 8, 8, 8), :]
            ya[e(0, 1, 0), 0:8, s] += gp[4 + h, pl.ds(base + 15, 8, 8), :]
            xa[e(-1, -1, 0), 15:16, s] += below[0, 0:1]
            xa[e(1, -1, 0), 7:8, s] += below[9, 0:1]
            xa[e(-1, 1, 0), 8:9, s] += above[0, 7:8]
            xa[e(1, 1, 0), 0:1, s] += above[9, 7:8]
        a = gp[6, pl.ds(base, 80)].reshape(10, 8, 128)
        below = pltpu.roll(a, 7, 1)
        above = pltpu.roll(gp[7, pl.ds(base, 80)].reshape(10, 8, 128), 1, 1)
        r = pltpu.roll(a, 64, 2) + jnp.where(y7, 0.0, below) + jnp.where(y0, 0.0, above)
        below = jnp.where(y7, below, 0.0)
        above = jnp.where(y0, above, 0.0)
        for jy, v in ((0, r), (-1, below), (1, above)):
            for jz in (-1, 1):
                w = jnp.where(low3 if jz < 0 else ~low3, v, 0.0)
                za[e(0, jy, jz)] += w[1:9].reshape(64, 128)
                za[e(-1, jy, jz), 56:64] += w[0]
                za[e(1, jy, jz), 0:8] += w[9]
        return carry

    lax.fori_loop(0, 8, brick, 0)
    for i in range(8):
        xg[i] = xa[i]
        yg[i] = ya[i]
        zg[i] = za[i]

    lane = iota((64, 128), 1)

    def put(out, at, n):
        entry = 8 + 2 * (n ^ 4)
        for k in range(2):
            xy = jnp.concatenate([xa[entry + k], ya[entry + k]], axis=0).astype(BF16)
            out[at, 64 * k : 64 * k + 32] = xy[:, :128]
            out[at, 64 * k + 32 : 64 * k + 64] = xy[:, 128:]
        out[at, 128:192] = jnp.where(lane < 64, za[entry], pltpu.roll(za[entry + 1], 64, 1)).astype(BF16)

    for n in range(4):
        put(first, n, 4 + n)
    put(first, 4, 0)
    for n in range(2):
        put(own_near, n, 1 + n)
    put(own_far, 0, 3)


def received(first, near, far, last):
    return [(last, 1), (last, 0), (far, 1), (far, 0), (first, 4), (near, 3), (near, 1), (last, 2)]


def taps_kernel(
    center, xf, yf, zf, entries, stack_t, first, near, far, last, taps, keep, give, xt, yt, zt, table, sem
):
    to_table = fetch((entries, table, sem.at[0]))[0]
    for i in range(8):
        xt[i] = xf[i]
        yt[i] = yf[i]
        zt[i] = zf[i]
    xt[DUMMY] = jnp.zeros((16, 256), F32)
    yt[DUMMY] = jnp.zeros((16, 256), F32)
    zt[DUMMY] = jnp.zeros((64, 128), F32)
    lane = iota((64, 128), 1)
    for n, (ref, at) in enumerate(received(first, near, far, last)):
        for k in range(2):
            entry = 8 + 2 * n + k
            for h in range(2):
                xy = ref[at, 64 * k + 32 * h : 64 * k + 32 * h + 32].astype(F32)
                xt[entry, :, 128 * h : 128 * h + 128] = xy[:16]
                yt[entry, :, 128 * h : 128 * h + 128] = xy[16:]
        z = ref[at, 128:192].astype(F32)
        turned = pltpu.roll(z, 64, 1)
        zt[8 + 2 * n] = jnp.where(lane < 64, z, turned)
        zt[9 + 2 * n] = jnp.where(lane < 64, turned, z)

    to_table.wait()
    low3 = (iota((8, 8, 128), 2) & 32) == 0
    low2 = (iota((8, 128), 1) & 32) == 0
    left3 = iota((10, 8, 128), 2) < 64

    def brick(b, carry):
        base = pl.multiple_of(80 * b, 16)
        e = lambda *j: table[b, col(*j)]
        y0, y7 = sublane_masks(10)
        for h in range(2):
            s = slice(128 * h, 128 * h + 128)
            r = jnp.concatenate(
                [
                    xt[e(-1, 0, 0), 8:16, s].reshape(1, 8, 128),
                    center[b, h].reshape(8, 8, 128),
                    xt[e(1, 0, 0), 0:8, s].reshape(1, 8, 128),
                ],
                axis=0,
            )

            def edge(jy, y_rows, x_row):
                first_row = xt[e(-1, jy, 0), 8 + x_row : 9 + x_row, s]
                last_row = xt[e(1, jy, 0), x_row : x_row + 1, s]
                entry = e(0, jy, 0)
                middle = [yt[entry, y_rows + x : y_rows + x + 1, s] for x in range(8)]
                rows = [first_row] + middle + [last_row]
                return jnp.stack([jnp.broadcast_to(row, (8, 128)) for row in rows], axis=0)

            below = jnp.where(y0, edge(-1, 8, 7), pltpu.roll(r, 1, 1))
            above = jnp.where(y7, edge(1, 0, 0), pltpu.roll(r, 7, 1))
            for n, v in enumerate((below, r, above)):
                taps[pl.ds(base, 80), 256 * n + 128 * h : 256 * n + 128 * h + 128] = v.reshape(80, 128).astype(BF16)

        def halo(jy):
            lo, hi = e(0, jy, -1), e(0, jy, 1)
            middle = jnp.where(low3, zt[lo].reshape(8, 8, 128), zt[hi].reshape(8, 8, 128))
            start = jnp.where(low2, zt[e(-1, jy, -1), 56:64], zt[e(-1, jy, 1), 56:64])
            end = jnp.where(low2, zt[e(1, jy, -1), 0:8], zt[e(1, jy, 1), 0:8])
            return jnp.concatenate([start[None], middle, end[None]], axis=0)

        r = halo(0)
        below = pltpu.roll(jnp.where(y7, halo(-1), r), 1, 1)
        above = pltpu.roll(jnp.where(y0, halo(1), r), 7, 1)
        taps[pl.ds(base, 80), 768:896] = jnp.where(left3, below, r).reshape(80, 128).astype(BF16)
        taps[pl.ds(base, 80), 896:1024] = jnp.where(left3, above, 0.0).reshape(80, 128).astype(BF16)
        return carry

    lax.fori_loop(0, 8, brick, 0)

    tap_lane = iota((32, 128), 1)
    pieces = []
    product = dot(stack_t[...], taps[...], NN)
    for dx in range(3):
        full = product[256 * dx : 256 * dx + 256]
        for dy in range(3):
            total = jnp.zeros((32, 128), F32)
            for z in range(8):
                rows = full[32 * z : 32 * z + 32]
                lo = rows[:, 256 * dy : 256 * dy + 128]
                hi = rows[:, 256 * dy + 128 : 256 * dy + 256]
                edge_tile = rows[:, 768 + 128 * (dy // 2) : 896 + 128 * (dy // 2)]
                at = 64 * (dy % 2)
                if z == 0:
                    v = jnp.where(tap_lane < 32, pltpu.roll(edge_tile, (128 - at) % 128, 1), pltpu.roll(lo, 32, 1))
                elif z == 7:
                    v = jnp.where(tap_lane < 64, pltpu.roll(hi, 64, 1), pltpu.roll(edge_tile, (32 - at) % 128, 1))
                else:
                    q = 32 * (z - 1)
                    left, right = (lo, lo) if q < 64 else (lo, hi) if q < 128 else (hi, hi)
                    if left is right:
                        v = pltpu.roll(left, (256 - q) % 128, 1) if q % 128 else left
                    else:
                        v = jnp.where(
                            tap_lane < 128 - q,
                            pltpu.roll(left, 128 - q, 1),
                            pltpu.roll(right, 128 - q, 1),
                        )
                total = total + v
            pieces.append(jnp.where(tap_lane < 96, total, 0.0))
    tiles = [jnp.zeros((32, 128), F32) for _ in range(7)]
    for n, piece in enumerate(pieces):
        start = 96 * n
        at, tile = start % 128, start // 128
        turned = pltpu.roll(piece, at, 1) if at else piece
        if at + 96 <= 128:
            tiles[tile] = tiles[tile] + turned
        else:
            tiles[tile] = tiles[tile] + jnp.where(tap_lane >= at, turned, 0.0)
            tiles[tile + 1] = tiles[tile + 1] + jnp.where(tap_lane < at, turned, 0.0)
    odd = parity() == 1
    for n in range(7):
        top, bottom = tiles[n][:16], tiles[n][16:]
        keep[:, 128 * n : 128 * n + 128] = jnp.where(odd, bottom, top)
        give[:, 128 * n : 128 * n + 128] = jnp.where(odd, top, bottom)


def conv_kernel(taps, wide, mask, conv):
    pre = jnp.zeros((8, 8, 8, 256), F32)
    for dx in range(3):
        u = dot(taps[...], wide[256 * dx : 256 * dx + 256], NT).reshape(8, 10, 8, 256)
        pre = pre + u[:, dx : dx + 8]
    by_z = swap_blocks([pre[b].reshape(64, 256) for b in range(8)])
    stacked = jnp.concatenate([v.astype(BF16) for v in by_z], axis=0)
    out = dot(stacked.T, voxel_order(), NN).reshape(8, 32, 512)
    conv[...] = (out * mask[...].astype(F32)[:, None, :]).astype(BF16)


def fold_kernel(center, xg, yg, zg, mask, send_hbm, first, near, far, last, out, xa, ya, za, send, sem):
    to_send = fetch((send_hbm, send, sem.at[0]))[0]
    flip = parity() * 4
    xa[...] = xg[...]
    ya[...] = yg[...]
    za[...] = zg[...]
    to_send.wait()
    for n, (ref, at) in enumerate(received(first, near, far, last)):
        u = n ^ 4 ^ flip
        z = ref[at, 128:192].astype(F32)
        for k in range(2):
            i = jnp.maximum(send[k, u], 0)
            for h in range(2):
                xy = ref[at, 64 * k + 32 * h : 64 * k + 32 * h + 32].astype(F32)
                xa[i, :, 128 * h : 128 * h + 128] += xy[:16]
                ya[i, :, 128 * h : 128 * h + 128] += xy[16:]
            za[i] += pltpu.roll(z, 64, 1) if k else z
    y0, y7 = sublane_masks(8)
    lane = iota((64, 128), 1)
    bricks = []
    for b in range(8):
        turned = pltpu.roll(za[b], 96, 1)
        halves = []
        for h in range(2):
            s = slice(128 * h, 128 * h + 128)
            c = center[b, h] + jnp.where(lane >= 96 if h else lane < 32, turned, 0.0)
            c = c.reshape(8, 8, 128)
            c = jnp.concatenate([c[0:1] + xa[b, 0:8, s][None], c[1:7], c[7:8] + xa[b, 8:16, s][None]], axis=0)
            low = jnp.stack([jnp.broadcast_to(ya[b, x : x + 1, s], (8, 128)) for x in range(8)], axis=0)
            high = jnp.stack([jnp.broadcast_to(ya[b, 8 + x : 9 + x, s], (8, 128)) for x in range(8)], axis=0)
            c = c + jnp.where(y0, low, 0.0) + jnp.where(y7, high, 0.0)
            halves.append(c.reshape(64, 128))
        bricks.append(jnp.concatenate(halves, axis=1))
    rows = jnp.concatenate(swap_blocks(bricks), axis=0).T
    coarse = rows.astype(BF16)
    fine = (rows - coarse.astype(F32)).astype(BF16)
    order = voxel_order()
    full = dot(coarse, order, NN) + dot(fine, order, NN)
    out[...] = full.reshape(8, 32, 512) * mask[...].astype(F32)[:, None, :]


def spread_kernel(scale, mine, other, out):
    odd = parity() == 1
    a, b = mine[...], other[...]
    wide = jnp.concatenate([jnp.where(odd, b, a), jnp.where(odd, a, b)], axis=0) * scale
    for t in range(27):
        at, tile = 32 * t % 128, 32 * t // 128
        v = wide[:, 128 * tile : 128 * tile + 128]
        v = pltpu.roll(v, 128 - at, 1) if at else v
        out[t] = v[:, :32]


def call(kernel, outs, scratch, ins, flops=0, size=0):
    return pl.pallas_call(
        kernel,
        out_shape=[jax.ShapeDtypeStruct(s, d) for s, d in outs],
        in_specs=ins,
        out_specs=[VMEM] * len(outs),
        scratch_shapes=scratch,
        compiler_params=pltpu.CompilerParams(vmem_limit_bytes=40 * 1024 * 1024),
        cost_estimate=pl.CostEstimate(flops=flops, bytes_accessed=size, transcendentals=0),
    )


def permute(value, target):
    count = lax.axis_size(RANGE_AXES)
    return lax.ppermute(value, RANGE_AXES, [(r, target(r, count)) for r in range(count)])


def in_hbm(value):
    return pltpu.with_memory_space_constraint(value, pltpu.HBM)


def swap(value, bit=1):
    return permute(value, lambda r, count: r ^ bit)


def onward(value, pairs, cross):
    return permute(value, lambda r, count: ((r + (-2 * pairs if r & 1 else 2 * pairs)) % count) ^ cross)


def exchange(first, near, far, later):
    near = jnp.concatenate([near, first[0:2]], axis=0)
    far = jnp.concatenate([far, first[2:4]], axis=0)
    near, far, later = lax.optimization_barrier((near, far, later))
    near = onward(near, 1, 1)
    far = onward(far, 2, 0)
    last = swap(jnp.concatenate([near[0:1], near[2:3], far[2:3]], axis=0))
    return (first, near, far, last), later


def body(features, voxel_mask, weights, grad_out, send_list, kernel_map):
    block = lambda n: ((n, BLOCK, 128), BF16)
    vm = lambda *shape: pltpu.VMEM(shape, F32)
    center_shape = ((8, 2, 64, 128), F32)
    face_shapes = [((8, 16, 256), F32), ((8, 16, 256), F32), ((8, 64, 128), F32)]
    accumulators = [vm(25, 16, 256), vm(25, 16, 256), vm(25, 64, 128)]
    values = [pltpu.VMEM((8, 32, 512), BF16), pltpu.VMEM((8, 512), jnp.int32)]
    send_space = pltpu.SMEM((2, 8), jnp.int32)
    table = pltpu.SMEM((8, 27), jnp.int32)
    sems = lambda n: pltpu.SemaphoreType.DMA((n,))
    send = in_hbm(send_list[0].T)

    first, own_near, own_far, center, xf, yf, zf = call(
        pack_kernel,
        [block(5), block(2), block(1), center_shape] + face_shapes,
        values + [send_space, sems(3)],
        [HBM] * 3,
        2 * 512 * 512 * 256,
        1 << 21,
    )(in_hbm(features), in_hbm(voxel_mask), send)
    got, kernel_map = exchange(swap(first), own_near, own_far, kernel_map)

    wide, stack_t, grad_center, xg, yg, zg, entries, grad_first, grad_near, grad_far = call(
        back_kernel,
        [((768, 1024), BF16), ((768, 640), BF16), center_shape]
        + face_shapes
        + [((8, 27), jnp.int32), block(5), block(2), block(1)],
        values
        + [pltpu.VMEM((27, 32, 32), BF16), pltpu.VMEM((8, 27), jnp.int32), pltpu.VMEM((640, 768), BF16), vm(8, 640, 128)]
        + accumulators
        + [table, sems(4)],
        [HBM] * 4,
        2 * 640 * 768 * 1024,
        8 << 20,
    )(*(in_hbm(v) for v in (grad_out, voxel_mask, weights, kernel_map)))

    taps, keep, give = call(
        taps_kernel,
        [((640, 1024), BF16), ((16, 896), F32), ((16, 896), F32)],
        accumulators + [table, sems(1)],
        [VMEM] * 10,
        2 * 640 * 768 * 1024,
        8 << 20,
    )(center, xf, yf, zf, entries, stack_t, *got)

    (conv,) = call(
        conv_kernel, [((8, 32, 512), BF16)], [], [VMEM] * 3, 2 * 640 * 768 * 1024, 4 << 20
    )(taps, wide, voxel_mask)

    grad_got, _ = exchange(swap(grad_first), grad_near, grad_far, 0.0)
    (grad_features,) = call(
        fold_kernel,
        [((8, 32, 512), F32)],
        [vm(8, 16, 256), vm(8, 16, 256), vm(8, 64, 128), send_space, sems(1)],
        [VMEM] * 5 + [HBM] + [VMEM] * 4,
        2 * 512 * 512 * 512,
        4 << 20,
    )(grad_center, xg, yg, zg, voxel_mask, send, *grad_got)

    part = keep + swap(give)
    bit = 2
    while bit < lax.axis_size(RANGE_AXES):
        other = swap(part, bit)
        if bit == 2:
            other, conv = lax.optimization_barrier((other, conv))
        if bit == 8:
            other, grad_features = lax.optimization_barrier((other, grad_features))
        part = part + other
        bit *= 2
    rest = swap(part)

    brick_count, _, voxels = features.shape
    scale = 1.0 / math.sqrt(brick_count * lax.axis_size(RANGE_AXES) * voxels)
    (grad_weights,) = call(functools.partial(spread_kernel, scale), [((27, 32, 32), F32)], [], [VMEM] * 2)(part, rest)
    return conv, grad_features, grad_weights


def solution(mesh):
    bricks = ("scene", "curve", "slab")
    return jax.shard_map(
        body,
        mesh=mesh,
        in_specs=(
            P(bricks, None, None),
            P(bricks, None),
            P(),
            P(bricks, None, None),
            P(bricks, None, None),
            P(bricks, None),
        ),
        out_specs=(
            P(bricks, None, None),
            P(bricks, None, None),
            P("scene", None, None),
        ),
        check_vma=False,
    )
```

```python
import functools
import math

import jax
import jax.numpy as jnp
from jax import lax
from jax.experimental import pallas as pl
from jax.experimental.pallas import tpu as pltpu
from jax.sharding import PartitionSpec as P

F32 = jnp.float32
BF16 = jnp.bfloat16
RANGE_AXES = ("curve", "slab")
VMEM = pl.BlockSpec(memory_space=pltpu.VMEM)
HBM = pl.BlockSpec(memory_space=pltpu.HBM)
NT = (((1,), (1,)), ((), ()))
NN = (((1,), (0,)), ((), ()))
TN = (((0,), (0,)), ((), ()))

BLOCK = 192
DUMMY = 24


def iota(shape, axis):
    return lax.broadcasted_iota(jnp.int32, shape, axis)


def dot(a, b, dims):
    return lax.dot_general(a, b, dims, preferred_element_type=F32)


def col(jx, jy, jz):
    return 9 * (jx + 1) + 3 * (jy + 1) + (jz + 1)


def voxel_order():
    row = iota((512, 512), 0)
    return jnp.where(iota((512, 512), 1) == ((row & 63) << 3) + (row >> 6), 1.0, 0.0).astype(BF16)


def swap_blocks(parts):
    lane = iota((64, 128), 1)
    half = [[p[:, :128], p[:, 128:]] for p in parts]
    now = [[half[(h << 2) | (i & 3)][i >> 2] for h in range(2)] for i in range(8)]
    for bit, shift in ((1, 64), (0, 32)):
        low = (lane & shift) == 0
        for i in range(8):
            if i >> bit & 1:
                continue
            j = i | (1 << bit)
            for h in range(2):
                p, q = now[i][h], now[j][h]
                now[i][h] = jnp.where(low, p, pltpu.roll(q, shift, 1))
                now[j][h] = jnp.where(low, pltpu.roll(p, 128 - shift, 1), q)
    return [jnp.concatenate(n, axis=1) for n in now]


def to_rows(values, order):
    swapped = dot(order, values, NT)
    return swap_blocks([swapped[64 * z : 64 * z + 64] for z in range(8)])


def masked_values(values, mask):
    return (values.astype(F32) * mask.astype(F32)[:, None, :]).astype(BF16).reshape(256, 512)


def parity():
    return (lax.axis_index("curve") * lax.axis_size("slab") + lax.axis_index("slab")) & 1


def fetch(*pairs):
    copies = [pltpu.make_async_copy(src, dst, sem) for src, dst, sem in pairs]
    for c in copies:
        c.start()
    return copies


def pack_kernel(feat_hbm, mask_hbm, send_hbm, first, own_near, own_far, center, xf, yf, zf, feat, mask, send, sems):
    copies = fetch((feat_hbm, feat, sems.at[0]), (mask_hbm, mask, sems.at[1]), (send_hbm, send, sems.at[2]))
    order = voxel_order()
    for c in copies:
        c.wait()
    bricks = to_rows(masked_values(feat[...], mask[...]), order)
    lane = iota((64, 128), 1)
    for b in range(8):
        c = bricks[b]
        for h in range(2):
            center[b, h] = c[:, 128 * h : 128 * h + 128]
        xf[b, 0:8] = c[0:8]
        xf[b, 8:16] = c[56:64]
        for h in range(2):
            s = slice(128 * h, 128 * h + 128)
            yf[b, 0:8, s] = center[b, h, pl.ds(0, 8, 8), :]
            yf[b, 8:16, s] = center[b, h, pl.ds(7, 8, 8), :]
        lo, hi = c[:, :128], c[:, 128:]
        even = jnp.where(lane < 64, pltpu.roll(hi, 32, 1), pltpu.roll(hi, 96, 1))
        odd = jnp.where(lane < 64, pltpu.roll(lo, 32, 1), pltpu.roll(lo, 96, 1))
        zf[b] = jnp.where((lane & 32) == 0, even, odd)
    flip = parity() * 4

    def put(out, at, u):
        pick = [jnp.maximum(send[k, u], 0) for k in range(2)]
        for k in range(2):
            xy = jnp.concatenate([xf[pick[k]], yf[pick[k]]], axis=0).astype(BF16)
            out[at, 64 * k : 64 * k + 32] = xy[:, :128]
            out[at, 64 * k + 32 : 64 * k + 64] = xy[:, 128:]
        out[at, 128:192] = jnp.where(lane < 64, zf[pick[0]], zf[pick[1]]).astype(BF16)

    for n in range(4):
        put(first, n, (4 + n) ^ flip)
    put(first, 4, flip)
    for n in range(2):
        put(own_near, n, (1 + n) ^ flip)
    put(own_far, 0, 3 ^ flip)


def sublane_masks(rows):
    y = iota((rows, 8, 128), 1)
    return y == 0, y == 7


def back_kernel(
    cot, mask, weights, kmap,
    wide, stack_t, center, xg, yg, zg, entries, first, own_near, own_far,
    stack, gp, xa, ya, za, table, sem,
):
    e = kmap[...]
    entries[...] = jnp.where(e < 0, DUMMY, jnp.where(e < 8, e, ((e - 8) ^ (parity() * 8)) + 8))
    to_table = fetch((entries, table, sem.at[0]))[0]
    order = voxel_order()
    tile = jnp.where((iota((32, 256), 1) & 31) == iota((32, 256), 0), 1.0, 0.0).astype(BF16)
    tiled = dot(weights[...].reshape(864, 32), tile, NN)
    block = iota((32, 256), 1) >> 5

    def tap(dx, dy, dz):
        t = col(dx - 1, dy - 1, dz - 1)
        return tiled[32 * t : 32 * t + 32]

    for dx in range(3):
        for z in range(8):
            rows = slice(256 * dx + 32 * z, 256 * dx + 32 * z + 32)
            for dy in range(3):
                w = jnp.zeros((32, 256), F32)
                for dz in range(3):
                    if 0 <= z + dz - 1 <= 7:
                        w = jnp.where(block == z + dz - 1, tap(dx, dy, dz), w)
                wide[rows, 256 * dy : 256 * dy + 256] = w.astype(BF16)
            w = jnp.zeros((32, 256), F32)
            if z in (0, 7):
                for dy in range(3):
                    w = jnp.where(block == 2 * dy + (z == 7), tap(dx, dy, 0 if z == 0 else 2), w)
            wide[rows, 768:1024] = w.astype(BF16)

    bricks = to_rows(masked_values(cot[...], mask[...]), order)
    for b in range(8):
        c = bricks[b]
        for d in range(3):
            before, after = jnp.zeros((8 * d, 256), F32), jnp.zeros((16 - 8 * d, 256), F32)
            pieces = [p for p in (before, c, after) if p.shape[0]]
            stack[80 * b : 80 * b + 80, 256 * d : 256 * d + 256] = jnp.concatenate(pieces, axis=0).astype(BF16)
    for d in range(3):
        stack_t[256 * d : 256 * d + 256] = stack[:, 256 * d : 256 * d + 256].T

    for n in range(4):
        s = slice(256 * n, 256 * n + 256)
        g = dot(stack[...], wide[:, s], NN)
        gp[2 * n] = g[:, :128]
        gp[2 * n + 1] = g[:, 128:]

    xa[...] = jnp.zeros_like(xa)
    ya[...] = jnp.zeros_like(ya)
    za[...] = jnp.zeros_like(za)
    to_table.wait()
    low3 = iota((10, 8, 128), 2) < 32

    def brick(b, carry):
        base = pl.multiple_of(80 * b, 80)
        e = lambda *j: table[b, col(*j)]
        y0, y7 = sublane_masks(10)
        for h in range(2):
            s = slice(128 * h, 128 * h + 128)

            def part(n):
                return gp[2 * n + h, pl.ds(base, 80)].reshape(10, 8, 128)

            below, above = part(0), part(2)
            r = (
                part(1)
                + jnp.where(y7, 0.0, pltpu.roll(below, 7, 1))
                + jnp.where(y0, 0.0, pltpu.roll(above, 1, 1))
            )
            center[b, h] = r[1:9].reshape(64, 128)
            xa[e(-1, 0, 0), 8:16, s] += r[0]
            xa[e(1, 0, 0), 0:8, s] += r[9]
            ya[e(0, -1, 0), 8:16, s] += gp[h, pl.ds(base + 8, 8, 8), :]
            ya[e(0, 1, 0), 0:8, s] += gp[4 + h, pl.ds(base + 15, 8, 8), :]
            xa[e(-1, -1, 0), 15:16, s] += below[0, 0:1]
            xa[e(1, -1, 0), 7:8, s] += below[9, 0:1]
            xa[e(-1, 1, 0), 8:9, s] += above[0, 7:8]
            xa[e(1, 1, 0), 0:1, s] += above[9, 7:8]
        a = gp[6, pl.ds(base, 80)].reshape(10, 8, 128)
        below = pltpu.roll(a, 7, 1)
        above = pltpu.roll(gp[7, pl.ds(base, 80)].reshape(10, 8, 128), 1, 1)
        r = pltpu.roll(a, 64, 2) + jnp.where(y7, 0.0, below) + jnp.where(y0, 0.0, above)
        below = jnp.where(y7, below, 0.0)
        above = jnp.where(y0, above, 0.0)
        for jy, v in ((0, r), (-1, below), (1, above)):
            for jz in (-1, 1):
                w = jnp.where(low3 if jz < 0 else ~low3, v, 0.0)
                za[e(0, jy, jz)] += w[1:9].reshape(64, 128)
                za[e(-1, jy, jz), 56:64] += w[0]
                za[e(1, jy, jz), 0:8] += w[9]
        return carry

    lax.fori_loop(0, 8, brick, 0, unroll=2)
    for i in range(8):
        xg[i] = xa[i]
        yg[i] = ya[i]
        zg[i] = za[i]

    lane = iota((64, 128), 1)

    def put(out, at, n):
        entry = 8 + 2 * (n ^ 4)
        for k in range(2):
            xy = jnp.concatenate([xa[entry + k], ya[entry + k]], axis=0).astype(BF16)
            out[at, 64 * k : 64 * k + 32] = xy[:, :128]
            out[at, 64 * k + 32 : 64 * k + 64] = xy[:, 128:]
        out[at, 128:192] = jnp.where(lane < 64, za[entry], pltpu.roll(za[entry + 1], 64, 1)).astype(BF16)

    for n in range(4):
        put(first, n, 4 + n)
    put(first, 4, 0)
    for n in range(2):
        put(own_near, n, 1 + n)
    put(own_far, 0, 3)


def received(first, near, far, last):
    return [(last, 1), (last, 0), (far, 1), (far, 0), (first, 4), (near, 3), (near, 1), (last, 2)]


def taps_kernel(
    center, xf, yf, zf, entries, stack_t, first, near, far, last, taps, keep, give, xt, yt, zt, table, sem
):
    to_table = fetch((entries, table, sem.at[0]))[0]
    for i in range(8):
        xt[i] = xf[i]
        yt[i] = yf[i]
        zt[i] = zf[i]
    xt[DUMMY] = jnp.zeros((16, 256), F32)
    yt[DUMMY] = jnp.zeros((16, 256), F32)
    zt[DUMMY] = jnp.zeros((64, 128), F32)
    lane = iota((64, 128), 1)
    for n, (ref, at) in enumerate(received(first, near, far, last)):
        for k in range(2):
            entry = 8 + 2 * n + k
            for h in range(2):
                xy = ref[at, 64 * k + 32 * h : 64 * k + 32 * h + 32].astype(F32)
                xt[entry, :, 128 * h : 128 * h + 128] = xy[:16]
                yt[entry, :, 128 * h : 128 * h + 128] = xy[16:]
        z = ref[at, 128:192].astype(F32)
        turned = pltpu.roll(z, 64, 1)
        zt[8 + 2 * n] = jnp.where(lane < 64, z, turned)
        zt[9 + 2 * n] = jnp.where(lane < 64, turned, z)

    to_table.wait()
    low3 = (iota((8, 8, 128), 2) & 32) == 0
    low2 = (iota((8, 128), 1) & 32) == 0
    left3 = iota((10, 8, 128), 2) < 64

    def brick(b, carry):
        base = pl.multiple_of(80 * b, 16)
        e = lambda *j: table[b, col(*j)]
        y0, y7 = sublane_masks(10)
        for h in range(2):
            s = slice(128 * h, 128 * h + 128)
            r = jnp.concatenate(
                [
                    xt[e(-1, 0, 0), 8:16, s].reshape(1, 8, 128),
                    center[b, h].reshape(8, 8, 128),
                    xt[e(1, 0, 0), 0:8, s].reshape(1, 8, 128),
                ],
                axis=0,
            )

            def edge(jy, y_rows, x_row):
                first_row = xt[e(-1, jy, 0), 8 + x_row : 9 + x_row, s]
                last_row = xt[e(1, jy, 0), x_row : x_row + 1, s]
                entry = e(0, jy, 0)
                middle = [yt[entry, y_rows + x : y_rows + x + 1, s] for x in range(8)]
                rows = [first_row] + middle + [last_row]
                return jnp.stack([jnp.broadcast_to(row, (8, 128)) for row in rows], axis=0)

            below = jnp.where(y0, edge(-1, 8, 7), pltpu.roll(r, 1, 1))
            above = jnp.where(y7, edge(1, 0, 0), pltpu.roll(r, 7, 1))
            for n, v in enumerate((below, r, above)):
                taps[pl.ds(base, 80), 256 * n + 128 * h : 256 * n + 128 * h + 128] = v.reshape(80, 128).astype(BF16)

        def halo(jy):
            lo, hi = e(0, jy, -1), e(0, jy, 1)
            middle = jnp.where(low3, zt[lo].reshape(8, 8, 128), zt[hi].reshape(8, 8, 128))
            start = jnp.where(low2, zt[e(-1, jy, -1), 56:64], zt[e(-1, jy, 1), 56:64])
            end = jnp.where(low2, zt[e(1, jy, -1), 0:8], zt[e(1, jy, 1), 0:8])
            return jnp.concatenate([start[None], middle, end[None]], axis=0)

        r = halo(0)
        below = pltpu.roll(jnp.where(y7, halo(-1), r), 1, 1)
        above = pltpu.roll(jnp.where(y0, halo(1), r), 7, 1)
        taps[pl.ds(base, 80), 768:896] = jnp.where(left3, below, r).reshape(80, 128).astype(BF16)
        taps[pl.ds(base, 80), 896:1024] = jnp.where(left3, above, 0.0).reshape(80, 128).astype(BF16)
        return carry

    lax.fori_loop(0, 8, brick, 0, unroll=8)

    tap_lane = iota((32, 128), 1)
    pieces = []
    product = dot(stack_t[...], taps[...], NN)
    for dx in range(3):
        full = product[256 * dx : 256 * dx + 256]
        for dy in range(3):
            total = jnp.zeros((32, 128), F32)
            for z in range(8):
                rows = full[32 * z : 32 * z + 32]
                lo = rows[:, 256 * dy : 256 * dy + 128]
                hi = rows[:, 256 * dy + 128 : 256 * dy + 256]
                edge_tile = rows[:, 768 + 128 * (dy // 2) : 896 + 128 * (dy // 2)]
                at = 64 * (dy % 2)
                if z == 0:
                    v = jnp.where(tap_lane < 32, pltpu.roll(edge_tile, (128 - at) % 128, 1), pltpu.roll(lo, 32, 1))
                elif z == 7:
                    v = jnp.where(tap_lane < 64, pltpu.roll(hi, 64, 1), pltpu.roll(edge_tile, (32 - at) % 128, 1))
                else:
                    q = 32 * (z - 1)
                    left, right = (lo, lo) if q < 64 else (lo, hi) if q < 128 else (hi, hi)
                    if left is right:
                        v = pltpu.roll(left, (256 - q) % 128, 1) if q % 128 else left
                    else:
                        v = jnp.where(
                            tap_lane < 128 - q,
                            pltpu.roll(left, 128 - q, 1),
                            pltpu.roll(right, 128 - q, 1),
                        )
                total = total + v
            pieces.append(jnp.where(tap_lane < 96, total, 0.0))
    tiles = [jnp.zeros((32, 128), F32) for _ in range(7)]
    for n, piece in enumerate(pieces):
        start = 96 * n
        at, tile = start % 128, start // 128
        turned = pltpu.roll(piece, at, 1) if at else piece
        if at + 96 <= 128:
            tiles[tile] = tiles[tile] + turned
        else:
            tiles[tile] = tiles[tile] + jnp.where(tap_lane >= at, turned, 0.0)
            tiles[tile + 1] = tiles[tile + 1] + jnp.where(tap_lane < at, turned, 0.0)
    odd = parity() == 1
    for n in range(7):
        top, bottom = tiles[n][:16], tiles[n][16:]
        keep[:, 128 * n : 128 * n + 128] = jnp.where(odd, bottom, top)
        give[:, 128 * n : 128 * n + 128] = jnp.where(odd, top, bottom)


def conv_kernel(taps, wide, mask, conv):
    pre = jnp.zeros((8, 8, 8, 256), F32)
    for dx in range(3):
        u = dot(taps[...], wide[256 * dx : 256 * dx + 256], NT).reshape(8, 10, 8, 256)
        pre = pre + u[:, dx : dx + 8]
    by_z = swap_blocks([pre[b].reshape(64, 256) for b in range(8)])
    stacked = jnp.concatenate([v.astype(BF16) for v in by_z], axis=0)
    out = dot(stacked.T, voxel_order(), NN).reshape(8, 32, 512)
    conv[...] = (out * mask[...].astype(F32)[:, None, :]).astype(BF16)


def fold_kernel(center, xg, yg, zg, mask, send_hbm, first, near, far, last, out, xa, ya, za, send, sem):
    to_send = fetch((send_hbm, send, sem.at[0]))[0]
    flip = parity() * 4
    xa[...] = xg[...]
    ya[...] = yg[...]
    za[...] = zg[...]
    to_send.wait()
    for n, (ref, at) in enumerate(received(first, near, far, last)):
        u = n ^ 4 ^ flip
        z = ref[at, 128:192].astype(F32)
        for k in range(2):
            i = jnp.maximum(send[k, u], 0)
            for h in range(2):
                xy = ref[at, 64 * k + 32 * h : 64 * k + 32 * h + 32].astype(F32)
                xa[i, :, 128 * h : 128 * h + 128] += xy[:16]
                ya[i, :, 128 * h : 128 * h + 128] += xy[16:]
            za[i] += pltpu.roll(z, 64, 1) if k else z
    y0, y7 = sublane_masks(8)
    lane = iota((64, 128), 1)
    bricks = []
    for b in range(8):
        turned = pltpu.roll(za[b], 96, 1)
        halves = []
        for h in range(2):
            s = slice(128 * h, 128 * h + 128)
            c = center[b, h] + jnp.where(lane >= 96 if h else lane < 32, turned, 0.0)
            c = c.reshape(8, 8, 128)
            c = jnp.concatenate([c[0:1] + xa[b, 0:8, s][None], c[1:7], c[7:8] + xa[b, 8:16, s][None]], axis=0)
            low = jnp.stack([jnp.broadcast_to(ya[b, x : x + 1, s], (8, 128)) for x in range(8)], axis=0)
            high = jnp.stack([jnp.broadcast_to(ya[b, 8 + x : 9 + x, s], (8, 128)) for x in range(8)], axis=0)
            c = c + jnp.where(y0, low, 0.0) + jnp.where(y7, high, 0.0)
            halves.append(c.reshape(64, 128))
        bricks.append(jnp.concatenate(halves, axis=1))
    rows = jnp.concatenate(swap_blocks(bricks), axis=0).T
    coarse = rows.astype(BF16)
    fine = (rows - coarse.astype(F32)).astype(BF16)
    order = voxel_order()
    full = dot(coarse, order, NN) + dot(fine, order, NN)
    out[...] = full.reshape(8, 32, 512) * mask[...].astype(F32)[:, None, :]


def spread_kernel(scale, mine, other, out):
    odd = parity() == 1
    a, b = mine[...], other[...]
    wide = jnp.concatenate([jnp.where(odd, b, a), jnp.where(odd, a, b)], axis=0) * scale
    for t in range(27):
        at, tile = 32 * t % 128, 32 * t // 128
        v = wide[:, 128 * tile : 128 * tile + 128]
        v = pltpu.roll(v, 128 - at, 1) if at else v
        out[t] = v[:, :32]


def call(kernel, outs, scratch, ins, flops=0, size=0):
    return pl.pallas_call(
        kernel,
        out_shape=[jax.ShapeDtypeStruct(s, d) for s, d in outs],
        in_specs=ins,
        out_specs=[VMEM] * len(outs),
        scratch_shapes=scratch,
        compiler_params=pltpu.CompilerParams(vmem_limit_bytes=40 * 1024 * 1024),
        cost_estimate=pl.CostEstimate(flops=flops, bytes_accessed=size, transcendentals=0),
    )


def permute(value, target):
    count = lax.axis_size(RANGE_AXES)
    return lax.ppermute(value, RANGE_AXES, [(r, target(r, count)) for r in range(count)])


def in_hbm(value):
    return pltpu.with_memory_space_constraint(value, pltpu.HBM)


def swap(value, bit=1):
    return permute(value, lambda r, count: r ^ bit)


def onward(value, pairs, cross):
    return permute(value, lambda r, count: ((r + (-2 * pairs if r & 1 else 2 * pairs)) % count) ^ cross)


def exchange(first, near, far, later):
    near = jnp.concatenate([near, first[0:2]], axis=0)
    far = jnp.concatenate([far, first[2:4]], axis=0)
    near, far, later = lax.optimization_barrier((near, far, later))
    return onward(near, 1, 1), onward(far, 2, 0), later


def exchange_end(near, far):
    return swap(jnp.concatenate([near[0:1], near[2:3], far[2:3]], axis=0))


def body(features, voxel_mask, weights, grad_out, send_list, kernel_map):
    block = lambda n: ((n, BLOCK, 128), BF16)
    vm = lambda *shape: pltpu.VMEM(shape, F32)
    center_shape = ((8, 2, 64, 128), F32)
    face_shapes = [((8, 16, 256), F32), ((8, 16, 256), F32), ((8, 64, 128), F32)]
    accumulators = [vm(25, 16, 256), vm(25, 16, 256), vm(25, 64, 128)]
    values = [pltpu.VMEM((8, 32, 512), BF16), pltpu.VMEM((8, 512), jnp.int32)]
    send_space = pltpu.SMEM((2, 8), jnp.int32)
    table = pltpu.SMEM((8, 27), jnp.int32)
    sems = lambda n: pltpu.SemaphoreType.DMA((n,))
    send = in_hbm(send_list[0].T)

    first, own_near, own_far, center, xf, yf, zf = call(
        pack_kernel,
        [block(5), block(2), block(1), center_shape] + face_shapes,
        values + [send_space, sems(3)],
        [HBM] * 3,
        2 * 512 * 512 * 256,
        1 << 21,
    )(in_hbm(features), in_hbm(voxel_mask), send)
    first = swap(first)
    near, far, kernel_map = exchange(first, own_near, own_far, kernel_map)
    last = exchange_end(near, far)

    wide, stack_t, grad_center, xg, yg, zg, entries, grad_first, grad_near, grad_far = call(
        back_kernel,
        [((768, 1024), BF16), ((768, 640), BF16), center_shape]
        + face_shapes
        + [((8, 27), jnp.int32), block(5), block(2), block(1)],
        [pltpu.VMEM((640, 768), BF16), vm(8, 640, 128)] + accumulators + [table, sems(1)],
        [VMEM] * 4,
        2 * 640 * 768 * 1024,
        8 << 20,
    )(grad_out, voxel_mask, weights, kernel_map)

    taps, keep, give = call(
        taps_kernel,
        [((640, 1024), BF16), ((16, 896), F32), ((16, 896), F32)],
        accumulators + [table, sems(1)],
        [VMEM] * 10,
    )(center, xf, yf, zf, entries, stack_t, first, near, far, last)

    (conv,) = call(
        conv_kernel, [((8, 32, 512), BF16)], [], [VMEM] * 3
    )(taps, wide, voxel_mask)

    grad_first = swap(grad_first)
    grad_near, grad_far, _ = exchange(grad_first, grad_near, grad_far, 0.0)

    part = keep + swap(give)
    other = swap(part, 2)
    other, conv, grad_near, grad_far = lax.optimization_barrier((other, conv, grad_near, grad_far))
    part = part + other
    grad_last = exchange_end(grad_near, grad_far)
    (grad_features,) = call(
        fold_kernel,
        [((8, 32, 512), F32)],
        [vm(8, 16, 256), vm(8, 16, 256), vm(8, 64, 128), send_space, sems(1)],
        [VMEM] * 5 + [HBM] + [VMEM] * 4,
    )(grad_center, xg, yg, zg, voxel_mask, send, grad_first, grad_near, grad_far, grad_last)

    bit = 4
    while bit < lax.axis_size(RANGE_AXES):
        other = swap(part, bit)
        if bit == 8:
            other, grad_features = lax.optimization_barrier((other, grad_features))
        part = part + other
        bit *= 2
    rest = swap(part)

    brick_count, _, voxels = features.shape
    scale = 1.0 / math.sqrt(brick_count * lax.axis_size(RANGE_AXES) * voxels)
    (grad_weights,) = call(functools.partial(spread_kernel, scale), [((27, 32, 32), F32)], [], [VMEM] * 2)(part, rest)
    return conv, grad_features, grad_weights


def solution(mesh):
    bricks = ("scene", "curve", "slab")
    return jax.shard_map(
        body,
        mesh=mesh,
        in_specs=(
            P(bricks, None, None),
            P(bricks, None),
            P(),
            P(bricks, None, None),
            P(bricks, None, None),
            P(bricks, None),
        ),
        out_specs=(
            P(bricks, None, None),
            P(bricks, None, None),
            P("scene", None, None),
        ),
        check_vma=False,
    )
```

```python
import functools
import math

import jax
import jax.numpy as jnp
from jax import lax
from jax.experimental import pallas as pl
from jax.experimental.pallas import tpu as pltpu
from jax.sharding import PartitionSpec as P

F32 = jnp.float32
BF16 = jnp.bfloat16
RANGE_AXES = ("curve", "slab")
VMEM = pl.BlockSpec(memory_space=pltpu.VMEM)
HBM = pl.BlockSpec(memory_space=pltpu.HBM)
NT = (((1,), (1,)), ((), ()))
NN = (((1,), (0,)), ((), ()))
TN = (((0,), (0,)), ((), ()))

BLOCK = 160
DUMMY = 24


def iota(shape, axis):
    return lax.broadcasted_iota(jnp.int32, shape, axis)


def dot(a, b, dims):
    return lax.dot_general(a, b, dims, preferred_element_type=F32)


def col(jx, jy, jz):
    return 9 * (jx + 1) + 3 * (jy + 1) + (jz + 1)


def voxel_order():
    row = iota((512, 512), 0)
    return jnp.where(iota((512, 512), 1) == ((row & 63) << 3) + (row >> 6), 1.0, 0.0).astype(BF16)


def swap_blocks(parts):
    lane = iota((64, 128), 1)
    half = [[p[:, :128], p[:, 128:]] for p in parts]
    now = [[half[(h << 2) | (i & 3)][i >> 2] for h in range(2)] for i in range(8)]
    for bit, shift in ((1, 64), (0, 32)):
        low = (lane & shift) == 0
        for i in range(8):
            if i >> bit & 1:
                continue
            j = i | (1 << bit)
            for h in range(2):
                p, q = now[i][h], now[j][h]
                now[i][h] = jnp.where(low, p, pltpu.roll(q, shift, 1))
                now[j][h] = jnp.where(low, pltpu.roll(p, 128 - shift, 1), q)
    return [jnp.concatenate(n, axis=1) for n in now]


def to_rows(values, order):
    swapped = dot(order, values, NT)
    return swap_blocks([swapped[64 * z : 64 * z + 64] for z in range(8)])


def masked_values(values, mask):
    return (values.astype(F32) * mask.astype(F32)[:, None, :]).astype(BF16).reshape(256, 512)


def parity():
    return (lax.axis_index("curve") * lax.axis_size("slab") + lax.axis_index("slab")) & 1


def fetch(*pairs):
    copies = [pltpu.make_async_copy(src, dst, sem) for src, dst, sem in pairs]
    for c in copies:
        c.start()
    return copies


def z_planes(lo, hi):
    lane = iota(lo.shape, 1)
    even = jnp.where(lane < 64, pltpu.roll(hi, 32, 1), pltpu.roll(hi, 96, 1))
    odd = jnp.where(lane < 64, pltpu.roll(lo, 32, 1), pltpu.roll(lo, 96, 1))
    return jnp.where((lane & 32) == 0, even, odd)


def half(h):
    return slice(128 * h, 128 * h + 128)


def put_block(out, at, x, y, z):
    for k in range(2):
        for h in range(2):
            row = 32 * k + 16 * h
            out[at, row : row + 16] = x[k][:, half(h)].astype(BF16)
    pieces = [y[k][a : a + 6, half(h)] for k in range(2) for h in range(2) for a in (1, 9)]
    out[at, 64:112] = jnp.concatenate(pieces, axis=0).astype(BF16)
    out[at, 112:160] = z.astype(BF16)


def get_block(ref, at):
    x = [[ref[at, 32 * k + 16 * h : 32 * k + 16 * h + 16].astype(F32) for h in range(2)] for k in range(2)]
    y = ref[at, 64:112].astype(F32)
    y = [[[y[24 * k + 12 * h + 6 * a :][:6] for a in range(2)] for h in range(2)] for k in range(2)]
    return x, y, ref[at, 112:160].astype(F32)


def pack_kernel(
    feat_hbm, mask_hbm, send_hbm, cot_hbm, weights_hbm, kmap_hbm,
    first, own_near, own_far, center, xf, yf, zf, mask, cot, weights, kmap,
    feat, send, sems,
):
    copies = fetch((feat_hbm, feat, sems.at[0]), (mask_hbm, mask, sems.at[1]), (send_hbm, send, sems.at[2]))
    later = fetch((cot_hbm, cot, sems.at[3]), (weights_hbm, weights, sems.at[4]), (kmap_hbm, kmap, sems.at[5]))
    order = voxel_order()
    for c in copies:
        c.wait()
    bricks = to_rows(masked_values(feat[...], mask[...]), order)
    lane = iota((48, 128), 1)
    for b in range(8):
        c = bricks[b]
        for h in range(2):
            center[b, h] = c[:, 128 * h : 128 * h + 128]
        xf[b, 0:8] = c[0:8]
        xf[b, 8:16] = c[56:64]
        for h in range(2):
            s = slice(128 * h, 128 * h + 128)
            yf[b, 0:8, s] = center[b, h, pl.ds(0, 8, 8), :]
            yf[b, 8:16, s] = center[b, h, pl.ds(7, 8, 8), :]
        zf[b] = z_planes(c[:, :128], c[:, 128:])
    flip = parity() * 4

    def put(out, at, u):
        pick = [jnp.maximum(send[k, u], 0) for k in range(2)]
        z = jnp.where(lane < 64, zf[pick[0], 8:56], zf[pick[1], 8:56])
        put_block(out, at, [xf[p] for p in pick], [yf[p] for p in pick], z)

    for n in range(4):
        put(first, n, (4 + n) ^ flip)
    put(first, 4, flip)
    for n in range(2):
        put(own_near, n, (1 + n) ^ flip)
    put(own_far, 0, 3 ^ flip)
    for c in later:
        c.wait()


def sublane_masks(rows):
    y = iota((rows, 8, 128), 1)
    return y == 0, y == 7


def back_kernel(
    cot, mask, weights, kmap,
    wide, keep_t, give_t, center, xg, yg, zg, entries, first, own_near, own_far,
    stack, gp, xa, ya, za, table, sem,
):
    e = kmap[...]
    entries[...] = jnp.where(e < 0, DUMMY, jnp.where(e < 8, e, ((e - 8) ^ (parity() * 8)) + 8))
    to_table = fetch((entries, table, sem.at[0]))[0]
    order = voxel_order()
    tile = jnp.where((iota((32, 256), 1) & 31) == iota((32, 256), 0), 1.0, 0.0).astype(BF16)
    tiled = dot(weights[...].reshape(864, 32), tile, NN)
    block = iota((32, 256), 1) >> 5

    def tap(dx, dy, dz):
        t = col(dx - 1, dy - 1, dz - 1)
        return tiled[32 * t : 32 * t + 32]

    for dx in range(3):
        for z in range(8):
            rows = slice(256 * dx + 32 * z, 256 * dx + 32 * z + 32)
            for dy in range(3):
                w = jnp.zeros((32, 256), F32)
                for dz in range(3):
                    if 0 <= z + dz - 1 <= 7:
                        w = jnp.where(block == z + dz - 1, tap(dx, dy, dz), w)
                wide[rows, 256 * dy : 256 * dy + 256] = w.astype(BF16)
            w = jnp.zeros((32, 256), F32)
            if z in (0, 7):
                for dy in range(3):
                    w = jnp.where(block == 2 * dy + (z == 7), tap(dx, dy, 0 if z == 0 else 2), w)
            wide[rows, 768:1024] = w.astype(BF16)

    bricks = to_rows(masked_values(cot[...], mask[...]), order)
    for b in range(8):
        c = bricks[b]
        for d in range(3):
            before, after = jnp.zeros((8 * d, 256), F32), jnp.zeros((16 - 8 * d, 256), F32)
            pieces = [p for p in (before, c, after) if p.shape[0]]
            stack[80 * b : 80 * b + 80, 256 * d : 256 * d + 256] = jnp.concatenate(pieces, axis=0).astype(BF16)
    odd = parity() == 1
    for d in range(3):
        turned = stack[:, 256 * d : 256 * d + 256].T.reshape(8, 2, 16, 640)
        top, bottom = turned[:, 0].reshape(128, 640), turned[:, 1].reshape(128, 640)
        keep_t[128 * d : 128 * d + 128] = jnp.where(odd, bottom, top)
        give_t[128 * d : 128 * d + 128] = jnp.where(odd, top, bottom)

    for n in range(4):
        s = slice(256 * n, 256 * n + 256)
        g = dot(stack[...], wide[:, s], NN)
        gp[2 * n] = g[:, :128]
        gp[2 * n + 1] = g[:, 128:]

    xa[...] = jnp.zeros_like(xa)
    ya[...] = jnp.zeros_like(ya)
    za[...] = jnp.zeros_like(za)
    to_table.wait()
    low3 = iota((10, 8, 128), 2) < 32

    def brick(b, carry):
        base = pl.multiple_of(80 * b, 80)
        e = lambda *j: table[b, col(*j)]
        y0, y7 = sublane_masks(10)
        for h in range(2):
            s = slice(128 * h, 128 * h + 128)

            def part(n):
                return gp[2 * n + h, pl.ds(base, 80)].reshape(10, 8, 128)

            below, above = part(0), part(2)
            r = (
                part(1)
                + jnp.where(y7, 0.0, pltpu.roll(below, 7, 1))
                + jnp.where(y0, 0.0, pltpu.roll(above, 1, 1))
            )
            center[b, h] = r[1:9].reshape(64, 128)
            xa[e(-1, 0, 0), 8:16, s] += r[0]
            xa[e(1, 0, 0), 0:8, s] += r[9]
            ya[e(0, -1, 0), 8:16, s] += gp[h, pl.ds(base + 8, 8, 8), :]
            ya[e(0, 1, 0), 0:8, s] += gp[4 + h, pl.ds(base + 15, 8, 8), :]
            xa[e(-1, -1, 0), 15:16, s] += below[0, 0:1]
            xa[e(1, -1, 0), 7:8, s] += below[9, 0:1]
            xa[e(-1, 1, 0), 8:9, s] += above[0, 7:8]
            xa[e(1, 1, 0), 0:1, s] += above[9, 7:8]
        a = gp[6, pl.ds(base, 80)].reshape(10, 8, 128)
        below = pltpu.roll(a, 7, 1)
        above = pltpu.roll(gp[7, pl.ds(base, 80)].reshape(10, 8, 128), 1, 1)
        r = pltpu.roll(a, 64, 2) + jnp.where(y7, 0.0, below) + jnp.where(y0, 0.0, above)
        below = jnp.where(y7, below, 0.0)
        above = jnp.where(y0, above, 0.0)
        for jy, v in ((0, r), (-1, below), (1, above)):
            for jz in (-1, 1):
                w = jnp.where(low3 if jz < 0 else ~low3, v, 0.0)
                za[e(0, jy, jz)] += w[1:9].reshape(64, 128)
                za[e(-1, jy, jz), 56:64] += w[0]
                za[e(1, jy, jz), 0:8] += w[9]
        return carry

    lax.fori_loop(0, 8, brick, 0, unroll=2)
    for i in range(8):
        xg[i] = xa[i]
        yg[i] = ya[i]
        zg[i] = za[i]

    lane = iota((48, 128), 1)
    edge_lane = iota((16, 128), 1)

    def put(out, at, n):
        entry = 8 + 2 * (n ^ 4)
        x, y = [], []
        for e in (entry, entry + 1):
            for row, from_row in ((0, 0), (7, 8), (8, 7), (15, 15)):
                xa[e, row : row + 1] += ya[e, from_row : from_row + 1]
            z = pltpu.roll(jnp.concatenate([za[e, 0:8], za[e, 56:64]], axis=0), 96, 1)
            lo = xa[e, :, :128] + jnp.where(edge_lane < 32, z, 0.0)
            hi = xa[e, :, 128:] + jnp.where(edge_lane >= 96, z, 0.0)
            x.append(jnp.concatenate([lo, hi], axis=1))
            y.append(ya[e])
        z = jnp.where(lane < 64, za[entry, 8:56], pltpu.roll(za[entry + 1, 8:56], 64, 1))
        put_block(out, at, x, y, z)

    for n in range(4):
        put(first, n, 4 + n)
    put(first, 4, 0)
    for n in range(2):
        put(own_near, n, 1 + n)
    put(own_far, 0, 3)


def received(first, near, far, last):
    return [(last, 1), (last, 0), (far, 1), (far, 0), (first, 4), (near, 3), (near, 1), (last, 2)]


def band_product(half_t, taps):
    product = dot(half_t, taps, NN)
    lane = iota((16, 128), 1)
    tiles = [jnp.zeros((16, 128), F32) for _ in range(7)]
    for n in range(9):
        dx, dy = n // 3, n % 3
        total = jnp.zeros((16, 128), F32)
        for z in range(8):
            rows = product[128 * dx + 16 * z : 128 * dx + 16 * z + 16]
            lo = rows[:, 256 * dy : 256 * dy + 128]
            hi = rows[:, 256 * dy + 128 : 256 * dy + 256]
            edge = rows[:, 768 + 128 * (dy // 2) : 896 + 128 * (dy // 2)]
            at = 64 * (dy % 2)
            if z == 0:
                v = jnp.where(lane < 32, pltpu.roll(edge, (128 - at) % 128, 1), pltpu.roll(lo, 32, 1))
            elif z == 7:
                v = jnp.where(lane < 64, pltpu.roll(hi, 64, 1), pltpu.roll(edge, (32 - at) % 128, 1))
            else:
                q = 32 * (z - 1)
                left, right = (lo, lo) if q < 64 else (lo, hi) if q < 128 else (hi, hi)
                if left is right:
                    v = pltpu.roll(left, (256 - q) % 128, 1) if q % 128 else left
                else:
                    v = jnp.where(lane < 128 - q, pltpu.roll(left, 128 - q, 1), pltpu.roll(right, 128 - q, 1))
            total = total + v
        piece = jnp.where(lane < 96, total, 0.0)
        at, tile = 96 * n % 128, 96 * n // 128
        turned = pltpu.roll(piece, at, 1) if at else piece
        if at + 96 <= 128:
            tiles[tile] = tiles[tile] + turned
        else:
            tiles[tile] = tiles[tile] + jnp.where(lane >= at, turned, 0.0)
            tiles[tile + 1] = tiles[tile + 1] + jnp.where(lane < at, turned, 0.0)
    return jnp.concatenate(tiles, axis=1)


def taps_kernel(
    center, xf, yf, zf, entries, give_t, first, near, far, last, taps, give, xt, yt, zt, table, sem
):
    to_table = fetch((entries, table, sem.at[0]))[0]
    for i in range(8):
        xt[i] = xf[i]
        yt[i] = yf[i]
        zt[i] = zf[i]
    xt[DUMMY] = jnp.zeros((16, 256), F32)
    yt[DUMMY] = jnp.zeros((16, 256), F32)
    zt[DUMMY] = jnp.zeros((64, 128), F32)
    lane = iota((48, 128), 1)
    for n, (ref, at) in enumerate(received(first, near, far, last)):
        x, y, z = get_block(ref, at)
        for k in range(2):
            entry = 8 + 2 * n + k
            for h in range(2):
                plane = x[k][h]
                xt[entry, :, half(h)] = plane
                yt[entry, 1:7, half(h)] = y[k][h][0]
                yt[entry, 9:15, half(h)] = y[k][h][1]
                for row, from_row in ((0, 0), (8, 7), (7, 8), (15, 15)):
                    yt[entry, row : row + 1, half(h)] = plane[from_row : from_row + 1]
            edges = z_planes(x[k][0], x[k][1])
            zt[entry, 0:8] = edges[0:8]
            zt[entry, 56:64] = edges[8:16]
        turned = pltpu.roll(z, 64, 1)
        zt[8 + 2 * n, 8:56] = jnp.where(lane < 64, z, turned)
        zt[9 + 2 * n, 8:56] = jnp.where(lane < 64, turned, z)

    to_table.wait()
    low3 = (iota((8, 8, 128), 2) & 32) == 0
    low2 = (iota((8, 128), 1) & 32) == 0
    left3 = iota((10, 8, 128), 2) < 64

    def brick(b, carry):
        base = pl.multiple_of(80 * b, 16)
        e = lambda *j: table[b, col(*j)]
        y0, y7 = sublane_masks(10)
        for h in range(2):
            s = slice(128 * h, 128 * h + 128)
            r = jnp.concatenate(
                [
                    xt[e(-1, 0, 0), 8:16, s].reshape(1, 8, 128),
                    center[b, h].reshape(8, 8, 128),
                    xt[e(1, 0, 0), 0:8, s].reshape(1, 8, 128),
                ],
                axis=0,
            )

            def edge(jy, y_rows, x_row):
                first_row = xt[e(-1, jy, 0), 8 + x_row : 9 + x_row, s]
                last_row = xt[e(1, jy, 0), x_row : x_row + 1, s]
                entry = e(0, jy, 0)
                middle = [yt[entry, y_rows + x : y_rows + x + 1, s] for x in range(8)]
                rows = [first_row] + middle + [last_row]
                return jnp.stack([jnp.broadcast_to(row, (8, 128)) for row in rows], axis=0)

            below = jnp.where(y0, edge(-1, 8, 7), pltpu.roll(r, 1, 1))
            above = jnp.where(y7, edge(1, 0, 0), pltpu.roll(r, 7, 1))
            for n, v in enumerate((below, r, above)):
                taps[pl.ds(base, 80), 256 * n + 128 * h : 256 * n + 128 * h + 128] = v.reshape(80, 128).astype(BF16)

        def halo(jy):
            lo, hi = e(0, jy, -1), e(0, jy, 1)
            middle = jnp.where(low3, zt[lo].reshape(8, 8, 128), zt[hi].reshape(8, 8, 128))
            start = jnp.where(low2, zt[e(-1, jy, -1), 56:64], zt[e(-1, jy, 1), 56:64])
            end = jnp.where(low2, zt[e(1, jy, -1), 0:8], zt[e(1, jy, 1), 0:8])
            return jnp.concatenate([start[None], middle, end[None]], axis=0)

        r = halo(0)
        below = pltpu.roll(jnp.where(y7, halo(-1), r), 1, 1)
        above = pltpu.roll(jnp.where(y0, halo(1), r), 7, 1)
        taps[pl.ds(base, 80), 768:896] = jnp.where(left3, below, r).reshape(80, 128).astype(BF16)
        taps[pl.ds(base, 80), 896:1024] = jnp.where(left3, above, 0.0).reshape(80, 128).astype(BF16)
        return carry

    lax.fori_loop(0, 8, brick, 0, unroll=8)

    give[...] = band_product(give_t[...], taps[...])


def keep_kernel(taps, keep_t, keep):
    keep[...] = band_product(keep_t[...], taps[...])


def conv_kernel(taps, wide, mask, conv):
    pre = jnp.zeros((8, 8, 8, 256), F32)
    for dx in range(3):
        u = dot(taps[...], wide[256 * dx : 256 * dx + 256], NT).reshape(8, 10, 8, 256)
        pre = pre + u[:, dx : dx + 8]
    by_z = swap_blocks([pre[b].reshape(64, 256) for b in range(8)])
    stacked = jnp.concatenate([v.astype(BF16) for v in by_z], axis=0)
    out = dot(stacked.T, voxel_order(), NN).reshape(8, 32, 512)
    conv[...] = (out * mask[...].astype(F32)[:, None, :]).astype(BF16)


def fold_kernel(center, xg, yg, zg, mask, send_hbm, first, near, far, last, out, xa, ya, za, send, sem):
    to_send = fetch((send_hbm, send, sem.at[0]))[0]
    flip = parity() * 4
    xa[...] = xg[...]
    ya[...] = yg[...]
    za[...] = zg[...]
    to_send.wait()
    for n, (ref, at) in enumerate(received(first, near, far, last)):
        u = n ^ 4 ^ flip
        x, y, z = get_block(ref, at)
        for k in range(2):
            i = jnp.maximum(send[k, u], 0)
            for h in range(2):
                xa[i, :, half(h)] += x[k][h]
                ya[i, 1:7, half(h)] += y[k][h][0]
                ya[i, 9:15, half(h)] += y[k][h][1]
            za[i, 8:56] += pltpu.roll(z, 64, 1) if k else z
    y0, y7 = sublane_masks(8)
    lane = iota((64, 128), 1)
    bricks = []
    for b in range(8):
        turned = pltpu.roll(za[b], 96, 1)
        halves = []
        for h in range(2):
            s = slice(128 * h, 128 * h + 128)
            c = center[b, h] + jnp.where(lane >= 96 if h else lane < 32, turned, 0.0)
            c = c.reshape(8, 8, 128)
            c = jnp.concatenate([c[0:1] + xa[b, 0:8, s][None], c[1:7], c[7:8] + xa[b, 8:16, s][None]], axis=0)
            low = jnp.stack([jnp.broadcast_to(ya[b, x : x + 1, s], (8, 128)) for x in range(8)], axis=0)
            high = jnp.stack([jnp.broadcast_to(ya[b, 8 + x : 9 + x, s], (8, 128)) for x in range(8)], axis=0)
            c = c + jnp.where(y0, low, 0.0) + jnp.where(y7, high, 0.0)
            halves.append(c.reshape(64, 128))
        bricks.append(jnp.concatenate(halves, axis=1))
    rows = jnp.concatenate(swap_blocks(bricks), axis=0).T
    coarse = rows.astype(BF16)
    fine = (rows - coarse.astype(F32)).astype(BF16)
    order = voxel_order()
    full = dot(coarse, order, NN) + dot(fine, order, NN)
    out[...] = full.reshape(8, 32, 512) * mask[...].astype(F32)[:, None, :]


def spread_kernel(scale, mine, other, out):
    odd = parity() == 1
    a, b = mine[...], other[...]
    wide = jnp.concatenate([jnp.where(odd, b, a), jnp.where(odd, a, b)], axis=0) * scale
    for t in range(27):
        at, tile = 32 * t % 128, 32 * t // 128
        v = wide[:, 128 * tile : 128 * tile + 128]
        v = pltpu.roll(v, 128 - at, 1) if at else v
        out[t] = v[:, :32]


def call(kernel, outs, scratch, ins, flops=0, size=0):
    return pl.pallas_call(
        kernel,
        out_shape=[jax.ShapeDtypeStruct(s, d) for s, d in outs],
        in_specs=ins,
        out_specs=[VMEM] * len(outs),
        scratch_shapes=scratch,
        compiler_params=pltpu.CompilerParams(vmem_limit_bytes=40 * 1024 * 1024),
        cost_estimate=pl.CostEstimate(flops=flops, bytes_accessed=size, transcendentals=0),
    )


def permute(value, target):
    count = lax.axis_size(RANGE_AXES)
    return lax.ppermute(value, RANGE_AXES, [(r, target(r, count)) for r in range(count)])


def in_hbm(value):
    return pltpu.with_memory_space_constraint(value, pltpu.HBM)


def swap(value, bit=1):
    return permute(value, lambda r, count: r ^ bit)


def onward(value, pairs, cross):
    return permute(value, lambda r, count: ((r + (-2 * pairs if r & 1 else 2 * pairs)) % count) ^ cross)


def exchange(first, near, far, later):
    near = jnp.concatenate([near, first[0:2]], axis=0)
    far = jnp.concatenate([far, first[2:4]], axis=0)
    near, far, later = lax.optimization_barrier((near, far, later))
    far = onward(far, 2, 0)
    return onward(near, 1, 1), far, later


def exchange_end(near, far):
    return swap(jnp.concatenate([near[0:1], near[2:3], far[2:3]], axis=0))


def body(features, voxel_mask, weights, grad_out, send_list, kernel_map):
    block = lambda n: ((n, BLOCK, 128), BF16)
    vm = lambda *shape: pltpu.VMEM(shape, F32)
    center_shape = ((8, 2, 64, 128), F32)
    face_shapes = [((8, 16, 256), F32), ((8, 16, 256), F32), ((8, 64, 128), F32)]
    accumulators = [vm(25, 16, 256), vm(25, 16, 256), vm(25, 64, 128)]
    send_space = pltpu.SMEM((2, 8), jnp.int32)
    table = pltpu.SMEM((8, 27), jnp.int32)
    sems = lambda n: pltpu.SemaphoreType.DMA((n,))
    send = in_hbm(send_list[0].T)

    first, own_near, own_far, center, xf, yf, zf, mask, cot, taps_w, kmap = call(
        pack_kernel,
        [block(5), block(2), block(1), center_shape]
        + face_shapes
        + [((8, 512), jnp.int32), ((8, 32, 512), BF16), ((27, 32, 32), BF16), ((8, 27), jnp.int32)],
        [pltpu.VMEM((8, 32, 512), BF16), send_space, sems(6)],
        [HBM] * 6,
        2 * 512 * 512 * 256,
        1 << 21,
    )(in_hbm(features), in_hbm(voxel_mask), send, in_hbm(grad_out), in_hbm(weights), in_hbm(kernel_map))
    first = swap(first)
    near, far, kmap = exchange(first, own_near, own_far, kmap)
    last = exchange_end(near, far)

    wide, keep_t, give_t, grad_center, xg, yg, zg, entries, grad_first, grad_near, grad_far = call(
        back_kernel,
        [((768, 1024), BF16), ((384, 640), BF16), ((384, 640), BF16), center_shape]
        + face_shapes
        + [((8, 27), jnp.int32), block(5), block(2), block(1)],
        [pltpu.VMEM((640, 768), BF16), vm(8, 640, 128)] + accumulators + [table, sems(1)],
        [VMEM] * 4,
        2 * 640 * 768 * 1024,
        8 << 20,
    )(cot, mask, taps_w, kmap)

    taps, give = call(
        taps_kernel,
        [((640, 1024), BF16), ((16, 896), F32)],
        accumulators + [table, sems(1)],
        [VMEM] * 10,
    )(center, xf, yf, zf, entries, give_t, first, near, far, last)

    (conv,) = call(
        conv_kernel, [((8, 32, 512), BF16)], [], [VMEM] * 3
    )(taps, wide, mask)

    grad_first = swap(grad_first)
    grad_near, grad_far, _ = exchange(grad_first, grad_near, grad_far, 0.0)

    (keep,) = call(keep_kernel, [((16, 896), F32)], [], [VMEM] * 2)(taps, keep_t)
    part = keep + swap(give)
    other = swap(part, 2)
    other, conv, grad_near, grad_far = lax.optimization_barrier((other, conv, grad_near, grad_far))
    part = part + other
    grad_last = exchange_end(grad_near, grad_far)
    (grad_features,) = call(
        fold_kernel,
        [((8, 32, 512), F32)],
        [vm(8, 16, 256), vm(8, 16, 256), vm(8, 64, 128), send_space, sems(1)],
        [VMEM] * 5 + [HBM] + [VMEM] * 4,
    )(grad_center, xg, yg, zg, mask, send, grad_first, grad_near, grad_far, grad_last)

    bit = 4
    while bit < lax.axis_size(RANGE_AXES):
        other = swap(part, bit)
        if bit == 8:
            other, grad_features = lax.optimization_barrier((other, grad_features))
        part = part + other
        bit *= 2
    rest = swap(part)

    brick_count, _, voxels = features.shape
    scale = 1.0 / math.sqrt(brick_count * lax.axis_size(RANGE_AXES) * voxels)
    (grad_weights,) = call(functools.partial(spread_kernel, scale), [((27, 32, 32), F32)], [], [VMEM] * 2)(part, rest)
    return conv, grad_features, grad_weights


def solution(mesh):
    bricks = ("scene", "curve", "slab")
    return jax.shard_map(
        body,
        mesh=mesh,
        in_specs=(
            P(bricks, None, None),
            P(bricks, None),
            P(),
            P(bricks, None, None),
            P(bricks, None, None),
            P(bricks, None),
        ),
        out_specs=(
            P(bricks, None, None),
            P(bricks, None, None),
            P("scene", None, None),
        ),
        check_vma=False,
    )
```

```python
import functools
import math

import jax
import jax.numpy as jnp
from jax import lax
from jax.experimental import pallas as pl
from jax.experimental.pallas import tpu as pltpu
from jax.sharding import PartitionSpec as P

F32 = jnp.float32
BF16 = jnp.bfloat16
RANGE_AXES = ("curve", "slab")
VMEM = pl.BlockSpec(memory_space=pltpu.VMEM)
HBM = pl.BlockSpec(memory_space=pltpu.HBM)
SMEM = pl.BlockSpec(memory_space=pltpu.SMEM)
NT = (((1,), (1,)), ((), ()))
NN = (((1,), (0,)), ((), ()))
TN = (((0,), (0,)), ((), ()))

BLOCK = 160
DUMMY = 24


def iota(shape, axis):
    return lax.broadcasted_iota(jnp.int32, shape, axis)


def dot(a, b, dims):
    return lax.dot_general(a, b, dims, preferred_element_type=F32)


def col(jx, jy, jz):
    return 9 * (jx + 1) + 3 * (jy + 1) + (jz + 1)


def voxel_order():
    row = iota((512, 512), 0)
    return jnp.where(iota((512, 512), 1) == ((row & 63) << 3) + (row >> 6), 1.0, 0.0).astype(BF16)


def swap_blocks(parts):
    lane = iota((64, 128), 1)
    half = [[p[:, :128], p[:, 128:]] for p in parts]
    now = [[half[(h << 2) | (i & 3)][i >> 2] for h in range(2)] for i in range(8)]
    for bit, shift in ((1, 64), (0, 32)):
        low = (lane & shift) == 0
        for i in range(8):
            if i >> bit & 1:
                continue
            j = i | (1 << bit)
            for h in range(2):
                p, q = now[i][h], now[j][h]
                now[i][h] = jnp.where(low, p, pltpu.roll(q, shift, 1))
                now[j][h] = jnp.where(low, pltpu.roll(p, 128 - shift, 1), q)
    return [jnp.concatenate(n, axis=1) for n in now]


def to_rows(values, order):
    swapped = dot(order, values, NT)
    return swap_blocks([swapped[64 * z : 64 * z + 64] for z in range(8)])


def masked_values(values, mask):
    return (values.astype(F32) * mask.astype(F32)[:, None, :]).astype(BF16).reshape(256, 512)


def parity():
    return (lax.axis_index("curve") * lax.axis_size("slab") + lax.axis_index("slab")) & 1


def fetch(*pairs):
    copies = [pltpu.make_async_copy(src, dst, sem) for src, dst, sem in pairs]
    for c in copies:
        c.start()
    return copies


def z_planes(lo, hi):
    lane = iota(lo.shape, 1)
    even = jnp.where(lane < 64, pltpu.roll(hi, 32, 1), pltpu.roll(hi, 96, 1))
    odd = jnp.where(lane < 64, pltpu.roll(lo, 32, 1), pltpu.roll(lo, 96, 1))
    return jnp.where((lane & 32) == 0, even, odd)


def half(h):
    return slice(128 * h, 128 * h + 128)


def put_block(out, at, x, y, z):
    for k in range(2):
        for h in range(2):
            row = 32 * k + 16 * h
            out[at, row : row + 16] = x[k][:, half(h)].astype(BF16)
    pieces = [y[k][a : a + 6, half(h)] for k in range(2) for h in range(2) for a in (1, 9)]
    out[at, 64:112] = jnp.concatenate(pieces, axis=0).astype(BF16)
    out[at, 112:160] = z.astype(BF16)


def get_block(ref, at):
    x = [[ref[at, 32 * k + 16 * h : 32 * k + 16 * h + 16].astype(F32) for h in range(2)] for k in range(2)]
    y = ref[at, 64:112].astype(F32)
    y = [[[y[24 * k + 12 * h + 6 * a :][:6] for a in range(2)] for h in range(2)] for k in range(2)]
    return x, y, ref[at, 112:160].astype(F32)


def pack_kernel(
    feat_hbm, mask_hbm, send_hbm, cot_hbm, weights_hbm, kmap_hbm,
    first, own_near, own_far, center, xf, yf, zf, mask, cot, weights, kmap,
    feat, send, sems,
):
    bricks = [(feat_hbm.at[pl.ds(b, 1)], feat.at[pl.ds(b, 1)], sems.at[5 + b]) for b in range(8)]
    copies = fetch(*bricks, (mask_hbm, mask, sems.at[0]), (send_hbm, send, sems.at[1]))
    later = fetch((cot_hbm, cot, sems.at[2]), (weights_hbm, weights, sems.at[3]), (kmap_hbm, kmap, sems.at[4]))
    order = voxel_order()
    for c in copies:
        c.wait()
    bricks = to_rows(masked_values(feat[...], mask[...]), order)
    lane = iota((48, 128), 1)
    for b in range(8):
        c = bricks[b]
        for h in range(2):
            center[b, h] = c[:, 128 * h : 128 * h + 128]
        xf[b, 0:8] = c[0:8]
        xf[b, 8:16] = c[56:64]
        for h in range(2):
            s = slice(128 * h, 128 * h + 128)
            yf[b, 0:8, s] = center[b, h, pl.ds(0, 8, 8), :]
            yf[b, 8:16, s] = center[b, h, pl.ds(7, 8, 8), :]
        zf[b] = z_planes(c[:, :128], c[:, 128:])
    flip = parity() * 4

    def put(out, at, u):
        pick = [jnp.maximum(send[k, u], 0) for k in range(2)]
        z = jnp.where(lane < 64, zf[pick[0], 8:56], zf[pick[1], 8:56])
        put_block(out, at, [xf[p] for p in pick], [yf[p] for p in pick], z)

    for n in range(4):
        put(first, n, (4 + n) ^ flip)
    put(first, 4, flip)
    for n in range(2):
        put(own_near, n, (1 + n) ^ flip)
    put(own_far, 0, 3 ^ flip)
    for c in later:
        c.wait()


def sublane_masks(rows):
    y = iota((rows, 8, 128), 1)
    return y == 0, y == 7


def stack_kernel(cot, mask, stack):
    order = voxel_order()
    bricks = to_rows(masked_values(cot[...], mask[...]), order)
    for b in range(8):
        c = bricks[b]
        for d in range(3):
            before, after = jnp.zeros((8 * d, 256), F32), jnp.zeros((16 - 8 * d, 256), F32)
            pieces = [p for p in (before, c, after) if p.shape[0]]
            stack[80 * b : 80 * b + 80, 256 * d : 256 * d + 256] = jnp.concatenate(pieces, axis=0).astype(BF16)


def back_kernel(
    stack, weights, kmap,
    wide, keep_t, give_t, center, xg, yg, zg, table, first, own_near, own_far,
    gp, xa, ya, za, entries, sem,
):
    e = kmap[...]
    entries[...] = jnp.where(e < 0, DUMMY, jnp.where(e < 8, e, ((e - 8) ^ (parity() * 8)) + 8))
    to_table = fetch((entries, table, sem.at[0]))[0]
    tile = jnp.where((iota((32, 256), 1) & 31) == iota((32, 256), 0), 1.0, 0.0).astype(BF16)
    tiled = dot(weights[...].reshape(864, 32), tile, NN)
    block = iota((32, 256), 1) >> 5

    def tap(dx, dy, dz):
        t = col(dx - 1, dy - 1, dz - 1)
        return tiled[32 * t : 32 * t + 32]

    for dx in range(3):
        for z in range(8):
            rows = slice(256 * dx + 32 * z, 256 * dx + 32 * z + 32)
            for dy in range(3):
                w = jnp.zeros((32, 256), F32)
                for dz in range(3):
                    if 0 <= z + dz - 1 <= 7:
                        w = jnp.where(block == z + dz - 1, tap(dx, dy, dz), w)
                wide[rows, 256 * dy : 256 * dy + 256] = w.astype(BF16)
            w = jnp.zeros((32, 256), F32)
            if z in (0, 7):
                for dy in range(3):
                    w = jnp.where(block == 2 * dy + (z == 7), tap(dx, dy, 0 if z == 0 else 2), w)
            wide[rows, 768:1024] = w.astype(BF16)

    odd = parity() == 1
    for d in range(3):
        turned = stack[:, 256 * d : 256 * d + 256].T.reshape(8, 2, 16, 640)
        top, bottom = turned[:, 0].reshape(128, 640), turned[:, 1].reshape(128, 640)
        keep_t[128 * d : 128 * d + 128] = jnp.where(odd, bottom, top)
        give_t[128 * d : 128 * d + 128] = jnp.where(odd, top, bottom)

    for n in range(4):
        s = slice(256 * n, 256 * n + 256)
        g = dot(stack[...], wide[:, s], NN)
        gp[2 * n] = g[:, :128]
        gp[2 * n + 1] = g[:, 128:]

    xa[...] = jnp.zeros_like(xa)
    ya[...] = jnp.zeros_like(ya)
    za[...] = jnp.zeros_like(za)
    to_table.wait()
    low3 = iota((10, 8, 128), 2) < 32

    def brick(b, carry):
        base = pl.multiple_of(80 * b, 80)
        e = lambda *j: table[b, col(*j)]
        y0, y7 = sublane_masks(10)
        for h in range(2):
            s = slice(128 * h, 128 * h + 128)

            def part(n):
                return gp[2 * n + h, pl.ds(base, 80)].reshape(10, 8, 128)

            below, above = part(0), part(2)
            r = (
                part(1)
                + jnp.where(y7, 0.0, pltpu.roll(below, 7, 1))
                + jnp.where(y0, 0.0, pltpu.roll(above, 1, 1))
            )
            center[b, h] = r[1:9].reshape(64, 128)
            xa[e(-1, 0, 0), 8:16, s] += r[0]
            xa[e(1, 0, 0), 0:8, s] += r[9]
            ya[e(0, -1, 0), 8:16, s] += gp[h, pl.ds(base + 8, 8, 8), :]
            ya[e(0, 1, 0), 0:8, s] += gp[4 + h, pl.ds(base + 15, 8, 8), :]
            xa[e(-1, -1, 0), 15:16, s] += below[0, 0:1]
            xa[e(1, -1, 0), 7:8, s] += below[9, 0:1]
            xa[e(-1, 1, 0), 8:9, s] += above[0, 7:8]
            xa[e(1, 1, 0), 0:1, s] += above[9, 7:8]
        a = gp[6, pl.ds(base, 80)].reshape(10, 8, 128)
        below = pltpu.roll(a, 7, 1)
        above = pltpu.roll(gp[7, pl.ds(base, 80)].reshape(10, 8, 128), 1, 1)
        r = pltpu.roll(a, 64, 2) + jnp.where(y7, 0.0, below) + jnp.where(y0, 0.0, above)
        below = jnp.where(y7, below, 0.0)
        above = jnp.where(y0, above, 0.0)
        for jy, v in ((0, r), (-1, below), (1, above)):
            for jz in (-1, 1):
                w = jnp.where(low3 if jz < 0 else ~low3, v, 0.0)
                za[e(0, jy, jz)] += w[1:9].reshape(64, 128)
                za[e(-1, jy, jz), 56:64] += w[0]
                za[e(1, jy, jz), 0:8] += w[9]
        return carry

    lax.fori_loop(0, 8, brick, 0, unroll=2)
    for i in range(8):
        xg[i] = xa[i]
        yg[i] = ya[i]
        zg[i] = za[i]

    lane = iota((48, 128), 1)
    edge_lane = iota((16, 128), 1)

    def put(out, at, n):
        entry = 8 + 2 * (n ^ 4)
        x, y = [], []
        for e in (entry, entry + 1):
            for row, from_row in ((0, 0), (7, 8), (8, 7), (15, 15)):
                xa[e, row : row + 1] += ya[e, from_row : from_row + 1]
            z = pltpu.roll(jnp.concatenate([za[e, 0:8], za[e, 56:64]], axis=0), 96, 1)
            lo = xa[e, :, :128] + jnp.where(edge_lane < 32, z, 0.0)
            hi = xa[e, :, 128:] + jnp.where(edge_lane >= 96, z, 0.0)
            x.append(jnp.concatenate([lo, hi], axis=1))
            y.append(ya[e])
        z = jnp.where(lane < 64, za[entry, 8:56], pltpu.roll(za[entry + 1, 8:56], 64, 1))
        put_block(out, at, x, y, z)

    for n in range(4):
        put(first, n, 4 + n)
    put(first, 4, 0)
    for n in range(2):
        put(own_near, n, 1 + n)
    put(own_far, 0, 3)


def received(first, near, far, last):
    return [(last, 1), (last, 0), (far, 1), (far, 0), (first, 4), (near, 3), (near, 1), (last, 2)]


def band_product(half_t, taps):
    product = dot(half_t, taps, NN)
    lane = iota((16, 128), 1)
    tiles = [jnp.zeros((16, 128), F32) for _ in range(7)]
    for n in range(9):
        dx, dy = n // 3, n % 3
        total = jnp.zeros((16, 128), F32)
        for z in range(8):
            rows = product[128 * dx + 16 * z : 128 * dx + 16 * z + 16]
            lo = rows[:, 256 * dy : 256 * dy + 128]
            hi = rows[:, 256 * dy + 128 : 256 * dy + 256]
            edge = rows[:, 768 + 128 * (dy // 2) : 896 + 128 * (dy // 2)]
            at = 64 * (dy % 2)
            if z == 0:
                v = jnp.where(lane < 32, pltpu.roll(edge, (128 - at) % 128, 1), pltpu.roll(lo, 32, 1))
            elif z == 7:
                v = jnp.where(lane < 64, pltpu.roll(hi, 64, 1), pltpu.roll(edge, (32 - at) % 128, 1))
            else:
                q = 32 * (z - 1)
                left, right = (lo, lo) if q < 64 else (lo, hi) if q < 128 else (hi, hi)
                if left is right:
                    v = pltpu.roll(left, (256 - q) % 128, 1) if q % 128 else left
                else:
                    v = jnp.where(lane < 128 - q, pltpu.roll(left, 128 - q, 1), pltpu.roll(right, 128 - q, 1))
            total = total + v
        piece = jnp.where(lane < 96, total, 0.0)
        at, tile = 96 * n % 128, 96 * n // 128
        turned = pltpu.roll(piece, at, 1) if at else piece
        if at + 96 <= 128:
            tiles[tile] = tiles[tile] + turned
        else:
            tiles[tile] = tiles[tile] + jnp.where(lane >= at, turned, 0.0)
            tiles[tile + 1] = tiles[tile + 1] + jnp.where(lane < at, turned, 0.0)
    return jnp.concatenate(tiles, axis=1)


def taps_kernel(
    center, xf, yf, zf, table, give_t, first, near, far, last, taps, give, xt, yt, zt
):
    for i in range(8):
        xt[i] = xf[i]
        yt[i] = yf[i]
        zt[i] = zf[i]
    xt[DUMMY] = jnp.zeros((16, 256), F32)
    yt[DUMMY] = jnp.zeros((16, 256), F32)
    zt[DUMMY] = jnp.zeros((64, 128), F32)
    lane = iota((48, 128), 1)
    for n, (ref, at) in enumerate(received(first, near, far, last)):
        x, y, z = get_block(ref, at)
        for k in range(2):
            entry = 8 + 2 * n + k
            for h in range(2):
                plane = x[k][h]
                xt[entry, :, half(h)] = plane
                yt[entry, 1:7, half(h)] = y[k][h][0]
                yt[entry, 9:15, half(h)] = y[k][h][1]
                for row, from_row in ((0, 0), (8, 7), (7, 8), (15, 15)):
                    yt[entry, row : row + 1, half(h)] = plane[from_row : from_row + 1]
            edges = z_planes(x[k][0], x[k][1])
            zt[entry, 0:8] = edges[0:8]
            zt[entry, 56:64] = edges[8:16]
        turned = pltpu.roll(z, 64, 1)
        zt[8 + 2 * n, 8:56] = jnp.where(lane < 64, z, turned)
        zt[9 + 2 * n, 8:56] = jnp.where(lane < 64, turned, z)

    low3 = (iota((8, 8, 128), 2) & 32) == 0
    low2 = (iota((8, 128), 1) & 32) == 0
    left3 = iota((10, 8, 128), 2) < 64

    def brick(b, carry):
        base = pl.multiple_of(80 * b, 16)
        e = lambda *j: table[b, col(*j)]
        y0, y7 = sublane_masks(10)
        for h in range(2):
            s = slice(128 * h, 128 * h + 128)
            r = jnp.concatenate(
                [
                    xt[e(-1, 0, 0), 8:16, s].reshape(1, 8, 128),
                    center[b, h].reshape(8, 8, 128),
                    xt[e(1, 0, 0), 0:8, s].reshape(1, 8, 128),
                ],
                axis=0,
            )

            def edge(jy, y_rows, x_row):
                first_row = xt[e(-1, jy, 0), 8 + x_row : 9 + x_row, s]
                last_row = xt[e(1, jy, 0), x_row : x_row + 1, s]
                entry = e(0, jy, 0)
                middle = [yt[entry, y_rows + x : y_rows + x + 1, s] for x in range(8)]
                rows = [first_row] + middle + [last_row]
                return jnp.stack([jnp.broadcast_to(row, (8, 128)) for row in rows], axis=0)

            below = jnp.where(y0, edge(-1, 8, 7), pltpu.roll(r, 1, 1))
            above = jnp.where(y7, edge(1, 0, 0), pltpu.roll(r, 7, 1))
            for n, v in enumerate((below, r, above)):
                taps[pl.ds(base, 80), 256 * n + 128 * h : 256 * n + 128 * h + 128] = v.reshape(80, 128).astype(BF16)

        def halo(jy):
            lo, hi = e(0, jy, -1), e(0, jy, 1)
            middle = jnp.where(low3, zt[lo].reshape(8, 8, 128), zt[hi].reshape(8, 8, 128))
            start = jnp.where(low2, zt[e(-1, jy, -1), 56:64], zt[e(-1, jy, 1), 56:64])
            end = jnp.where(low2, zt[e(1, jy, -1), 0:8], zt[e(1, jy, 1), 0:8])
            return jnp.concatenate([start[None], middle, end[None]], axis=0)

        r = halo(0)
        below = pltpu.roll(jnp.where(y7, halo(-1), r), 1, 1)
        above = pltpu.roll(jnp.where(y0, halo(1), r), 7, 1)
        taps[pl.ds(base, 80), 768:896] = jnp.where(left3, below, r).reshape(80, 128).astype(BF16)
        taps[pl.ds(base, 80), 896:1024] = jnp.where(left3, above, 0.0).reshape(80, 128).astype(BF16)
        return carry

    lax.fori_loop(0, 8, brick, 0, unroll=8)

    give[...] = band_product(give_t[...], taps[...])


def keep_kernel(taps, keep_t, keep):
    keep[...] = band_product(keep_t[...], taps[...])


def conv_kernel(taps, wide, mask, conv):
    pre = jnp.zeros((8, 8, 8, 256), F32)
    for dx in range(3):
        u = dot(taps[...], wide[256 * dx : 256 * dx + 256], NT).reshape(8, 10, 8, 256)
        pre = pre + u[:, dx : dx + 8]
    by_z = swap_blocks([pre[b].reshape(64, 256) for b in range(8)])
    stacked = jnp.concatenate([v.astype(BF16) for v in by_z], axis=0)
    out = dot(stacked.T, voxel_order(), NN).reshape(8, 32, 512)
    conv[...] = (out * mask[...].astype(F32)[:, None, :]).astype(BF16)


def fold_kernel(center, xg, yg, zg, mask, send_hbm, first, near, far, last, out, xa, ya, za, send, sem):
    to_send = fetch((send_hbm, send, sem.at[0]))[0]
    flip = parity() * 4
    xa[...] = xg[...]
    ya[...] = yg[...]
    za[...] = zg[...]
    to_send.wait()
    for n, (ref, at) in enumerate(received(first, near, far, last)):
        u = n ^ 4 ^ flip
        x, y, z = get_block(ref, at)
        for k in range(2):
            i = jnp.maximum(send[k, u], 0)
            for h in range(2):
                xa[i, :, half(h)] += x[k][h]
                ya[i, 1:7, half(h)] += y[k][h][0]
                ya[i, 9:15, half(h)] += y[k][h][1]
            za[i, 8:56] += pltpu.roll(z, 64, 1) if k else z
    y0, y7 = sublane_masks(8)
    lane = iota((64, 128), 1)
    bricks = []
    for b in range(8):
        turned = pltpu.roll(za[b], 96, 1)
        halves = []
        for h in range(2):
            s = slice(128 * h, 128 * h + 128)
            c = center[b, h] + jnp.where(lane >= 96 if h else lane < 32, turned, 0.0)
            c = c.reshape(8, 8, 128)
            c = jnp.concatenate([c[0:1] + xa[b, 0:8, s][None], c[1:7], c[7:8] + xa[b, 8:16, s][None]], axis=0)
            low = jnp.stack([jnp.broadcast_to(ya[b, x : x + 1, s], (8, 128)) for x in range(8)], axis=0)
            high = jnp.stack([jnp.broadcast_to(ya[b, 8 + x : 9 + x, s], (8, 128)) for x in range(8)], axis=0)
            c = c + jnp.where(y0, low, 0.0) + jnp.where(y7, high, 0.0)
            halves.append(c.reshape(64, 128))
        bricks.append(jnp.concatenate(halves, axis=1))
    rows = jnp.concatenate(swap_blocks(bricks), axis=0).T
    coarse = rows.astype(BF16)
    fine = (rows - coarse.astype(F32)).astype(BF16)
    order = voxel_order()
    full = dot(coarse, order, NN) + dot(fine, order, NN)
    out[...] = full.reshape(8, 32, 512) * mask[...].astype(F32)[:, None, :]


def spread_kernel(scale, mine, other, out):
    odd = parity() == 1
    a, b = mine[...], other[...]
    wide = jnp.concatenate([jnp.where(odd, b, a), jnp.where(odd, a, b)], axis=0) * scale
    for t in range(27):
        at, tile = 32 * t % 128, 32 * t // 128
        v = wide[:, 128 * tile : 128 * tile + 128]
        v = pltpu.roll(v, 128 - at, 1) if at else v
        out[t] = v[:, :32]


def call(kernel, outs, scratch, ins, flops=0, size=0):
    return pl.pallas_call(
        kernel,
        out_shape=[jax.ShapeDtypeStruct(*o) if isinstance(o, tuple) else o for o in outs],
        in_specs=ins,
        out_specs=[VMEM if isinstance(o, tuple) else SMEM for o in outs],
        scratch_shapes=scratch,
        compiler_params=pltpu.CompilerParams(vmem_limit_bytes=40 * 1024 * 1024),
        cost_estimate=pl.CostEstimate(flops=flops, bytes_accessed=size, transcendentals=0),
    )


def permute(value, target):
    count = lax.axis_size(RANGE_AXES)
    return lax.ppermute(value, RANGE_AXES, [(r, target(r, count)) for r in range(count)])


def in_hbm(value):
    return pltpu.with_memory_space_constraint(value, pltpu.HBM)


def swap(value, bit=1):
    return permute(value, lambda r, count: r ^ bit)


def onward(value, pairs, cross):
    return permute(value, lambda r, count: ((r + (-2 * pairs if r & 1 else 2 * pairs)) % count) ^ cross)


def exchange(first, near, far, *later):
    near = jnp.concatenate([near, first[0:2]], axis=0)
    far = jnp.concatenate([far, first[2:4]], axis=0)
    near, far, *later = lax.optimization_barrier((near, far, *later))
    near = onward(near, 1, 1)
    return near, onward(far, 2, 0), *later


def exchange_end(near, far):
    return swap(jnp.concatenate([near[0:1], near[2:3], far[2:3]], axis=0))


def body(features, voxel_mask, weights, grad_out, send_list, kernel_map):
    block = lambda n: ((n, BLOCK, 128), BF16)
    vm = lambda *shape: pltpu.VMEM(shape, F32)
    center_shape = ((8, 2, 64, 128), F32)
    face_shapes = [((8, 16, 256), F32), ((8, 16, 256), F32), ((8, 64, 128), F32)]
    accumulators = [vm(25, 16, 256), vm(25, 16, 256), vm(25, 64, 128)]
    send_space = pltpu.SMEM((2, 8), jnp.int32)
    sems = lambda n: pltpu.SemaphoreType.DMA((n,))
    send = in_hbm(send_list[0].T)

    first, own_near, own_far, center, xf, yf, zf, mask, cot, taps_w, kmap = call(
        pack_kernel,
        [block(5), block(2), block(1), center_shape]
        + face_shapes
        + [((8, 512), jnp.int32), ((8, 32, 512), BF16), ((27, 32, 32), BF16), ((8, 27), jnp.int32)],
        [pltpu.VMEM((8, 32, 512), BF16), send_space, sems(13)],
        [HBM] * 6,
        2 * 512 * 512 * 256,
        1 << 21,
    )(in_hbm(features), in_hbm(voxel_mask), send, in_hbm(grad_out), in_hbm(weights), in_hbm(kernel_map))
    first = swap(first)
    (stack,) = call(stack_kernel, [((640, 768), BF16)], [], [VMEM] * 2, 1 << 28, 2 << 20)(cot, mask)
    near, far, kmap, stack = exchange(first, own_near, own_far, kmap, stack)
    last = exchange_end(near, far)

    wide, keep_t, give_t, grad_center, xg, yg, zg, table, grad_first, grad_near, grad_far = call(
        back_kernel,
        [((768, 1024), BF16), ((384, 640), BF16), ((384, 640), BF16), center_shape]
        + face_shapes
        + [pltpu.SMEM((8, 27), jnp.int32), block(5), block(2), block(1)],
        [vm(8, 640, 128)] + accumulators + [pltpu.VMEM((8, 27), jnp.int32), sems(1)],
        [VMEM] * 3,
        2 * 640 * 768 * 1024,
        8 << 20,
    )(stack, taps_w, kmap)

    taps, give = call(
        taps_kernel,
        [((640, 1024), BF16), ((16, 896), F32)],
        accumulators,
        [VMEM] * 4 + [SMEM] + [VMEM] * 5,
    )(center, xf, yf, zf, pltpu.with_memory_space_constraint(table, pltpu.SMEM), give_t, first, near, far, last)

    (conv,) = call(
        conv_kernel, [((8, 32, 512), BF16)], [], [VMEM] * 3
    )(taps, wide, mask)

    grad_first = swap(grad_first)
    grad_near, grad_far = exchange(grad_first, grad_near, grad_far)

    (keep,) = call(keep_kernel, [((16, 896), F32)], [], [VMEM] * 2)(taps, keep_t)
    part = keep + swap(give)
    other = swap(part, 2)
    other, conv, grad_near, grad_far = lax.optimization_barrier((other, conv, grad_near, grad_far))
    part = part + other
    grad_last = exchange_end(grad_near, grad_far)
    (grad_features,) = call(
        fold_kernel,
        [((8, 32, 512), F32)],
        [vm(8, 16, 256), vm(8, 16, 256), vm(8, 64, 128), send_space, sems(1)],
        [VMEM] * 5 + [HBM] + [VMEM] * 4,
    )(grad_center, xg, yg, zg, mask, send, grad_first, grad_near, grad_far, grad_last)

    bit = 4
    while bit < lax.axis_size(RANGE_AXES):
        other = swap(part, bit)
        if bit == 8:
            other, grad_features = lax.optimization_barrier((other, grad_features))
        part = part + other
        bit *= 2
    rest = swap(part)

    brick_count, _, voxels = features.shape
    scale = 1.0 / math.sqrt(brick_count * lax.axis_size(RANGE_AXES) * voxels)
    (grad_weights,) = call(functools.partial(spread_kernel, scale), [((27, 32, 32), F32)], [], [VMEM] * 2)(part, rest)
    return conv, grad_features, grad_weights


def solution(mesh):
    bricks = ("scene", "curve", "slab")
    return jax.shard_map(
        body,
        mesh=mesh,
        in_specs=(
            P(bricks, None, None),
            P(bricks, None),
            P(),
            P(bricks, None, None),
            P(bricks, None, None),
            P(bricks, None),
        ),
        out_specs=(
            P(bricks, None, None),
            P(bricks, None, None),
            P("scene", None, None),
        ),
        check_vma=False,
    )
```

```python
import functools
import math

import jax
import jax.numpy as jnp
from jax import lax
from jax.experimental import pallas as pl
from jax.experimental.pallas import tpu as pltpu
from jax.sharding import PartitionSpec as P

F32 = jnp.float32
BF16 = jnp.bfloat16
RANGE_AXES = ("curve", "slab")
VMEM = pl.BlockSpec(memory_space=pltpu.VMEM)
HBM = pl.BlockSpec(memory_space=pltpu.HBM)
SMEM = pl.BlockSpec(memory_space=pltpu.SMEM)
NT = (((1,), (1,)), ((), ()))
NN = (((1,), (0,)), ((), ()))
TN = (((0,), (0,)), ((), ()))

BLOCK = 160
DUMMY = 24


def iota(shape, axis):
    return lax.broadcasted_iota(jnp.int32, shape, axis)


def dot(a, b, dims):
    return lax.dot_general(a, b, dims, preferred_element_type=F32)


def col(jx, jy, jz):
    return 9 * (jx + 1) + 3 * (jy + 1) + (jz + 1)


def voxel_order():
    row = iota((512, 512), 0)
    return jnp.where(iota((512, 512), 1) == ((row & 63) << 3) + (row >> 6), 1.0, 0.0).astype(BF16)


def swap_blocks(parts):
    lane = iota((64, 128), 1)
    half = [[p[:, :128], p[:, 128:]] for p in parts]
    now = [[half[(h << 2) | (i & 3)][i >> 2] for h in range(2)] for i in range(8)]
    for bit, shift in ((1, 64), (0, 32)):
        low = (lane & shift) == 0
        for i in range(8):
            if i >> bit & 1:
                continue
            j = i | (1 << bit)
            for h in range(2):
                p, q = now[i][h], now[j][h]
                now[i][h] = jnp.where(low, p, pltpu.roll(q, shift, 1))
                now[j][h] = jnp.where(low, pltpu.roll(p, 128 - shift, 1), q)
    return [jnp.concatenate(n, axis=1) for n in now]


def to_rows(values, order):
    swapped = dot(order, values, NT)
    return swap_blocks([swapped[64 * z : 64 * z + 64] for z in range(8)])


def masked_values(values, mask):
    return (values.astype(F32) * mask.astype(F32)[:, None, :]).astype(BF16).reshape(256, 512)


def parity():
    return (lax.axis_index("curve") * lax.axis_size("slab") + lax.axis_index("slab")) & 1


def fetch(*pairs):
    copies = [pltpu.make_async_copy(src, dst, sem) for src, dst, sem in pairs]
    for c in copies:
        c.start()
    return copies


def z_planes(lo, hi):
    lane = iota(lo.shape, 1)
    even = jnp.where(lane < 64, pltpu.roll(hi, 32, 1), pltpu.roll(hi, 96, 1))
    odd = jnp.where(lane < 64, pltpu.roll(lo, 32, 1), pltpu.roll(lo, 96, 1))
    return jnp.where((lane & 32) == 0, even, odd)


def half(h):
    return slice(128 * h, 128 * h + 128)


def put_block(out, at, x, y, z):
    for k in range(2):
        for h in range(2):
            row = 32 * k + 16 * h
            out[at, row : row + 16] = x[k][:, half(h)].astype(BF16)
    pieces = [y[k][a : a + 6, half(h)] for k in range(2) for h in range(2) for a in (1, 9)]
    out[at, 64:112] = jnp.concatenate(pieces, axis=0).astype(BF16)
    out[at, 112:160] = z.astype(BF16)


def get_block(ref, at):
    x = [[ref[at, 32 * k + 16 * h : 32 * k + 16 * h + 16].astype(F32) for h in range(2)] for k in range(2)]
    y = ref[at, 64:112].astype(F32)
    y = [[[y[24 * k + 12 * h + 6 * a :][:6] for a in range(2)] for h in range(2)] for k in range(2)]
    return x, y, ref[at, 112:160].astype(F32)


def pack_kernel(
    feat_hbm, mask_hbm, send_hbm, cot_hbm, weights_hbm, kmap_hbm,
    first, own_near, own_far, center, xf, yf, zf, mask, cot, weights, kmap,
    feat, send, padded, sems,
):
    bricks = [(feat_hbm.at[pl.ds(b, 1)], feat.at[pl.ds(b, 1)], sems.at[5 + b]) for b in range(8)]
    copies = fetch(*bricks, (mask_hbm, mask, sems.at[0]), (send_hbm, send, sems.at[1]))
    later = fetch((cot_hbm, cot, sems.at[2]), (weights_hbm, weights, sems.at[3]), (kmap_hbm, kmap, sems.at[4]))
    order = voxel_order()
    for c in copies:
        c.wait()
    bricks = to_rows(masked_values(feat[...], mask[...]), order)
    lane = iota((48, 128), 1)
    for b in range(8):
        c = bricks[b]
        for h in range(2):
            center[b, h] = c[:, 128 * h : 128 * h + 128]
            padded[b, h, 0:64] = c[:, 128 * h : 128 * h + 128]
        xf[b, 0:8] = c[0:8]
        xf[b, 8:16] = c[56:64]
        for h in range(2):
            s = slice(128 * h, 128 * h + 128)
            yf[b, 0:8, s] = padded[b, h, pl.ds(0, 8, 8), :]
            yf[b, 8:16, s] = padded[b, h, pl.ds(7, 8, 8), :]
        zf[b] = z_planes(c[:, :128], c[:, 128:])
    flip = parity() * 4

    def put(out, at, u):
        pick = [jnp.maximum(send[k, u], 0) for k in range(2)]
        z = jnp.where(lane < 64, zf[pick[0], 8:56], zf[pick[1], 8:56])
        put_block(out, at, [xf[p] for p in pick], [yf[p] for p in pick], z)

    for n in range(4):
        put(first, n, (4 + n) ^ flip)
    put(first, 4, flip)
    for n in range(2):
        put(own_near, n, (1 + n) ^ flip)
    put(own_far, 0, 3 ^ flip)
    for c in later:
        c.wait()


def sublane_masks(rows):
    y = iota((rows, 8, 128), 1)
    return y == 0, y == 7


def stack_kernel(cot, mask, stack):
    order = voxel_order()
    bricks = to_rows(masked_values(cot[...], mask[...]), order)
    for b in range(8):
        c = bricks[b]
        for d in range(3):
            before, after = jnp.zeros((8 * d, 256), F32), jnp.zeros((16 - 8 * d, 256), F32)
            pieces = [p for p in (before, c, after) if p.shape[0]]
            stack[80 * b : 80 * b + 80, 256 * d : 256 * d + 256] = jnp.concatenate(pieces, axis=0).astype(BF16)


def back_kernel(
    stack, weights, kmap,
    wide, keep_t, give_t, center, xg, yg, zg, table, first, own_near, own_far,
    gp, xa, ya, za, entries, sem,
):
    e = kmap[...]
    entries[...] = jnp.where(e < 0, DUMMY, jnp.where(e < 8, e, ((e - 8) ^ (parity() * 8)) + 8))
    to_table = fetch((entries, table, sem.at[0]))[0]
    tile = jnp.where((iota((32, 256), 1) & 31) == iota((32, 256), 0), 1.0, 0.0).astype(BF16)
    tiled = dot(weights[...].reshape(864, 32), tile, NN)
    block = iota((32, 256), 1) >> 5

    def tap(dx, dy, dz):
        t = col(dx - 1, dy - 1, dz - 1)
        return tiled[32 * t : 32 * t + 32]

    for dx in range(3):
        for z in range(8):
            rows = slice(256 * dx + 32 * z, 256 * dx + 32 * z + 32)
            for dy in range(3):
                w = jnp.zeros((32, 256), F32)
                for dz in range(3):
                    if 0 <= z + dz - 1 <= 7:
                        w = jnp.where(block == z + dz - 1, tap(dx, dy, dz), w)
                wide[rows, 256 * dy : 256 * dy + 256] = w.astype(BF16)
            w = jnp.zeros((32, 256), F32)
            if z in (0, 7):
                for dy in range(3):
                    w = jnp.where(block == 2 * dy + (z == 7), tap(dx, dy, 0 if z == 0 else 2), w)
            wide[rows, 768:1024] = w.astype(BF16)

    odd = parity() == 1
    for d in range(3):
        turned = stack[:, 256 * d : 256 * d + 256].T.reshape(8, 2, 16, 640)
        top, bottom = turned[:, 0].reshape(128, 640), turned[:, 1].reshape(128, 640)
        keep_t[128 * d : 128 * d + 128] = jnp.where(odd, bottom, top)
        give_t[128 * d : 128 * d + 128] = jnp.where(odd, top, bottom)

    for n in range(4):
        s = slice(256 * n, 256 * n + 256)
        g = dot(stack[...], wide[:, s], NN)
        gp[2 * n] = g[:, :128]
        gp[2 * n + 1] = g[:, 128:]

    xa[...] = jnp.zeros_like(xa)
    ya[...] = jnp.zeros_like(ya)
    za[...] = jnp.zeros_like(za)
    to_table.wait()
    low3 = iota((10, 8, 128), 2) < 32

    def brick(b, carry):
        base = pl.multiple_of(80 * b, 80)
        e = lambda *j: table[b, col(*j)]
        y0, y7 = sublane_masks(10)
        for h in range(2):
            s = slice(128 * h, 128 * h + 128)

            def part(n):
                return gp[2 * n + h, pl.ds(base, 80)].reshape(10, 8, 128)

            below, above = part(0), part(2)
            r = (
                part(1)
                + jnp.where(y7, 0.0, pltpu.roll(below, 7, 1))
                + jnp.where(y0, 0.0, pltpu.roll(above, 1, 1))
            )
            center[b, h] = r[1:9].reshape(64, 128)
            xa[e(-1, 0, 0), 8:16, s] += r[0]
            xa[e(1, 0, 0), 0:8, s] += r[9]
            ya[e(0, -1, 0), 8:16, s] += gp[h, pl.ds(base + 8, 8, 8), :]
            ya[e(0, 1, 0), 0:8, s] += gp[4 + h, pl.ds(base + 15, 8, 8), :]
            xa[e(-1, -1, 0), 15:16, s] += below[0, 0:1]
            xa[e(1, -1, 0), 7:8, s] += below[9, 0:1]
            xa[e(-1, 1, 0), 8:9, s] += above[0, 7:8]
            xa[e(1, 1, 0), 0:1, s] += above[9, 7:8]
        a = gp[6, pl.ds(base, 80)].reshape(10, 8, 128)
        below = pltpu.roll(a, 7, 1)
        above = pltpu.roll(gp[7, pl.ds(base, 80)].reshape(10, 8, 128), 1, 1)
        r = pltpu.roll(a, 64, 2) + jnp.where(y7, 0.0, below) + jnp.where(y0, 0.0, above)
        below = jnp.where(y7, below, 0.0)
        above = jnp.where(y0, above, 0.0)
        for jy, v in ((0, r), (-1, below), (1, above)):
            for jz in (-1, 1):
                w = jnp.where(low3 if jz < 0 else ~low3, v, 0.0)
                za[e(0, jy, jz)] += w[1:9].reshape(64, 128)
                za[e(-1, jy, jz), 56:64] += w[0]
                za[e(1, jy, jz), 0:8] += w[9]
        return carry

    lax.fori_loop(0, 8, brick, 0, unroll=2)
    for i in range(8):
        xg[i] = xa[i]
        yg[i] = ya[i]
        zg[i] = za[i]

    lane = iota((48, 128), 1)
    edge_lane = iota((16, 128), 1)

    def put(out, at, n):
        entry = 8 + 2 * (n ^ 4)
        x, y = [], []
        for e in (entry, entry + 1):
            for row, from_row in ((0, 0), (7, 8), (8, 7), (15, 15)):
                xa[e, row : row + 1] += ya[e, from_row : from_row + 1]
            z = pltpu.roll(jnp.concatenate([za[e, 0:8], za[e, 56:64]], axis=0), 96, 1)
            lo = xa[e, :, :128] + jnp.where(edge_lane < 32, z, 0.0)
            hi = xa[e, :, 128:] + jnp.where(edge_lane >= 96, z, 0.0)
            x.append(jnp.concatenate([lo, hi], axis=1))
            y.append(ya[e])
        z = jnp.where(lane < 64, za[entry, 8:56], pltpu.roll(za[entry + 1, 8:56], 64, 1))
        put_block(out, at, x, y, z)

    for n in range(4):
        put(first, n, 4 + n)
    put(first, 4, 0)
    for n in range(2):
        put(own_near, n, 1 + n)
    put(own_far, 0, 3)


def received(first, near, far, last):
    return [(last, 1), (last, 0), (far, 1), (far, 0), (first, 4), (near, 3), (near, 1), (last, 2)]


def band_product(half_t, taps):
    product = dot(half_t, taps, NN)
    lane = iota((16, 128), 1)
    tiles = [jnp.zeros((16, 128), F32) for _ in range(7)]
    for n in range(9):
        dx, dy = n // 3, n % 3
        total = jnp.zeros((16, 128), F32)
        for z in range(8):
            rows = product[128 * dx + 16 * z : 128 * dx + 16 * z + 16]
            lo = rows[:, 256 * dy : 256 * dy + 128]
            hi = rows[:, 256 * dy + 128 : 256 * dy + 256]
            edge = rows[:, 768 + 128 * (dy // 2) : 896 + 128 * (dy // 2)]
            at = 64 * (dy % 2)
            if z == 0:
                v = jnp.where(lane < 32, pltpu.roll(edge, (128 - at) % 128, 1), pltpu.roll(lo, 32, 1))
            elif z == 7:
                v = jnp.where(lane < 64, pltpu.roll(hi, 64, 1), pltpu.roll(edge, (32 - at) % 128, 1))
            else:
                q = 32 * (z - 1)
                left, right = (lo, lo) if q < 64 else (lo, hi) if q < 128 else (hi, hi)
                if left is right:
                    v = pltpu.roll(left, (256 - q) % 128, 1) if q % 128 else left
                else:
                    v = jnp.where(lane < 128 - q, pltpu.roll(left, 128 - q, 1), pltpu.roll(right, 128 - q, 1))
            total = total + v
        piece = jnp.where(lane < 96, total, 0.0)
        at, tile = 96 * n % 128, 96 * n // 128
        turned = pltpu.roll(piece, at, 1) if at else piece
        if at + 96 <= 128:
            tiles[tile] = tiles[tile] + turned
        else:
            tiles[tile] = tiles[tile] + jnp.where(lane >= at, turned, 0.0)
            tiles[tile + 1] = tiles[tile + 1] + jnp.where(lane < at, turned, 0.0)
    return jnp.concatenate(tiles, axis=1)


def taps_kernel(
    center, xf, yf, zf, table, give_t, first, near, far, last, taps, give, xt, yt, zt
):
    for i in range(8):
        xt[i] = xf[i]
        yt[i] = yf[i]
        zt[i] = zf[i]
    xt[DUMMY] = jnp.zeros((16, 256), F32)
    yt[DUMMY] = jnp.zeros((16, 256), F32)
    zt[DUMMY] = jnp.zeros((64, 128), F32)
    lane = iota((48, 128), 1)
    for n, (ref, at) in enumerate(received(first, near, far, last)):
        x, y, z = get_block(ref, at)
        for k in range(2):
            entry = 8 + 2 * n + k
            for h in range(2):
                plane = x[k][h]
                xt[entry, :, half(h)] = plane
                yt[entry, 1:7, half(h)] = y[k][h][0]
                yt[entry, 9:15, half(h)] = y[k][h][1]
                for row, from_row in ((0, 0), (8, 7), (7, 8), (15, 15)):
                    yt[entry, row : row + 1, half(h)] = plane[from_row : from_row + 1]
            edges = z_planes(x[k][0], x[k][1])
            zt[entry, 0:8] = edges[0:8]
            zt[entry, 56:64] = edges[8:16]
        turned = pltpu.roll(z, 64, 1)
        zt[8 + 2 * n, 8:56] = jnp.where(lane < 64, z, turned)
        zt[9 + 2 * n, 8:56] = jnp.where(lane < 64, turned, z)

    low3 = (iota((8, 8, 128), 2) & 32) == 0
    low2 = (iota((8, 128), 1) & 32) == 0
    left3 = iota((10, 8, 128), 2) < 64

    def brick(b, carry):
        base = pl.multiple_of(80 * b, 16)
        e = lambda *j: table[b, col(*j)]
        y0, y7 = sublane_masks(10)
        for h in range(2):
            s = slice(128 * h, 128 * h + 128)
            r = jnp.concatenate(
                [
                    xt[e(-1, 0, 0), 8:16, s].reshape(1, 8, 128),
                    center[b, h].reshape(8, 8, 128),
                    xt[e(1, 0, 0), 0:8, s].reshape(1, 8, 128),
                ],
                axis=0,
            )

            def edge(jy, y_rows, x_row):
                first_row = xt[e(-1, jy, 0), 8 + x_row : 9 + x_row, s]
                last_row = xt[e(1, jy, 0), x_row : x_row + 1, s]
                entry = e(0, jy, 0)
                middle = [yt[entry, y_rows + x : y_rows + x + 1, s] for x in range(8)]
                rows = [first_row] + middle + [last_row]
                return jnp.stack([jnp.broadcast_to(row, (8, 128)) for row in rows], axis=0)

            below = jnp.where(y0, edge(-1, 8, 7), pltpu.roll(r, 1, 1))
            above = jnp.where(y7, edge(1, 0, 0), pltpu.roll(r, 7, 1))
            for n, v in enumerate((below, r, above)):
                taps[pl.ds(base, 80), 256 * n + 128 * h : 256 * n + 128 * h + 128] = v.reshape(80, 128).astype(BF16)

        def halo(jy):
            lo, hi = e(0, jy, -1), e(0, jy, 1)
            middle = jnp.where(low3, zt[lo].reshape(8, 8, 128), zt[hi].reshape(8, 8, 128))
            start = jnp.where(low2, zt[e(-1, jy, -1), 56:64], zt[e(-1, jy, 1), 56:64])
            end = jnp.where(low2, zt[e(1, jy, -1), 0:8], zt[e(1, jy, 1), 0:8])
            return jnp.concatenate([start[None], middle, end[None]], axis=0)

        r = halo(0)
        below = pltpu.roll(jnp.where(y7, halo(-1), r), 1, 1)
        above = pltpu.roll(jnp.where(y0, halo(1), r), 7, 1)
        taps[pl.ds(base, 80), 768:896] = jnp.where(left3, below, r).reshape(80, 128).astype(BF16)
        taps[pl.ds(base, 80), 896:1024] = jnp.where(left3, above, 0.0).reshape(80, 128).astype(BF16)
        return carry

    lax.fori_loop(0, 8, brick, 0, unroll=8)

    give[...] = band_product(give_t[...], taps[...])


def keep_kernel(taps, keep_t, keep):
    keep[...] = band_product(keep_t[...], taps[...])


def conv_kernel(taps, wide, mask, conv):
    pre = jnp.zeros((8, 8, 8, 256), F32)
    for dx in range(3):
        u = dot(taps[...], wide[256 * dx : 256 * dx + 256], NT).reshape(8, 10, 8, 256)
        pre = pre + u[:, dx : dx + 8]
    by_z = swap_blocks([pre[b].reshape(64, 256) for b in range(8)])
    stacked = jnp.concatenate([v.astype(BF16) for v in by_z], axis=0)
    out = dot(stacked.T, voxel_order(), NN).reshape(8, 32, 512)
    conv[...] = (out * mask[...].astype(F32)[:, None, :]).astype(BF16)


def fold_kernel(center, xg, yg, zg, mask, send_hbm, first, near, far, last, out, xa, ya, za, send, sem):
    to_send = fetch((send_hbm, send, sem.at[0]))[0]
    flip = parity() * 4
    xa[...] = xg[...]
    ya[...] = yg[...]
    za[...] = zg[...]
    to_send.wait()
    for n, (ref, at) in enumerate(received(first, near, far, last)):
        u = n ^ 4 ^ flip
        x, y, z = get_block(ref, at)
        for k in range(2):
            i = jnp.maximum(send[k, u], 0)
            for h in range(2):
                xa[i, :, half(h)] += x[k][h]
                ya[i, 1:7, half(h)] += y[k][h][0]
                ya[i, 9:15, half(h)] += y[k][h][1]
            za[i, 8:56] += pltpu.roll(z, 64, 1) if k else z
    y0, y7 = sublane_masks(8)
    lane = iota((64, 128), 1)
    bricks = []
    for b in range(8):
        turned = pltpu.roll(za[b], 96, 1)
        halves = []
        for h in range(2):
            s = slice(128 * h, 128 * h + 128)
            c = center[b, h] + jnp.where(lane >= 96 if h else lane < 32, turned, 0.0)
            c = c.reshape(8, 8, 128)
            c = jnp.concatenate([c[0:1] + xa[b, 0:8, s][None], c[1:7], c[7:8] + xa[b, 8:16, s][None]], axis=0)
            low = jnp.stack([jnp.broadcast_to(ya[b, x : x + 1, s], (8, 128)) for x in range(8)], axis=0)
            high = jnp.stack([jnp.broadcast_to(ya[b, 8 + x : 9 + x, s], (8, 128)) for x in range(8)], axis=0)
            c = c + jnp.where(y0, low, 0.0) + jnp.where(y7, high, 0.0)
            halves.append(c.reshape(64, 128))
        bricks.append(jnp.concatenate(halves, axis=1))
    rows = jnp.concatenate(swap_blocks(bricks), axis=0).T
    coarse = rows.astype(BF16)
    fine = (rows - coarse.astype(F32)).astype(BF16)
    order = voxel_order()
    full = dot(coarse, order, NN) + dot(fine, order, NN)
    out[...] = full.reshape(8, 32, 512) * mask[...].astype(F32)[:, None, :]


def spread_kernel(scale, mine, other, out):
    odd = parity() == 1
    a, b = mine[...], other[...]
    wide = jnp.concatenate([jnp.where(odd, b, a), jnp.where(odd, a, b)], axis=0) * scale
    for t in range(27):
        at, tile = 32 * t % 128, 32 * t // 128
        v = wide[:, 128 * tile : 128 * tile + 128]
        v = pltpu.roll(v, 128 - at, 1) if at else v
        out[t] = v[:, :32]


def call(kernel, outs, scratch, ins, flops=0, size=0):
    return pl.pallas_call(
        kernel,
        out_shape=[jax.ShapeDtypeStruct(*o) if isinstance(o, tuple) else o for o in outs],
        in_specs=ins,
        out_specs=[VMEM if isinstance(o, tuple) else SMEM for o in outs],
        scratch_shapes=scratch,
        compiler_params=pltpu.CompilerParams(vmem_limit_bytes=40 * 1024 * 1024),
        cost_estimate=pl.CostEstimate(flops=flops, bytes_accessed=size, transcendentals=0),
    )


def permute(value, target):
    count = lax.axis_size(RANGE_AXES)
    return lax.ppermute(value, RANGE_AXES, [(r, target(r, count)) for r in range(count)])


def in_hbm(value):
    return pltpu.with_memory_space_constraint(value, pltpu.HBM)


def swap(value, bit=1):
    return permute(value, lambda r, count: r ^ bit)


def onward(value, pairs, cross):
    return permute(value, lambda r, count: ((r + (-2 * pairs if r & 1 else 2 * pairs)) % count) ^ cross)


def exchange(first, near, far, *later):
    near = jnp.concatenate([near, first[0:2]], axis=0)
    far = jnp.concatenate([far, first[2:4]], axis=0)
    near, far, *later = lax.optimization_barrier((near, far, *later))
    near = onward(near, 1, 1)
    return near, onward(far, 2, 0), *later


def exchange_end(near, far):
    return swap(jnp.concatenate([near[0:1], near[2:3], far[2:3]], axis=0))


def body(features, voxel_mask, weights, grad_out, send_list, kernel_map):
    block = lambda n: ((n, BLOCK, 128), BF16)
    vm = lambda *shape: pltpu.VMEM(shape, F32)
    center_shape = ((8, 2, 64, 128), F32)
    face_shapes = [((8, 16, 256), F32), ((8, 16, 256), F32), ((8, 64, 128), F32)]
    accumulators = [vm(25, 16, 256), vm(25, 16, 256), vm(25, 64, 128)]
    send_space = pltpu.SMEM((2, 8), jnp.int32)
    sems = lambda n: pltpu.SemaphoreType.DMA((n,))
    send = in_hbm(send_list[0].T)

    first, own_near, own_far, center, xf, yf, zf, mask, cot, taps_w, kmap = call(
        pack_kernel,
        [block(5), block(2), block(1), center_shape]
        + face_shapes
        + [((8, 512), jnp.int32), ((8, 32, 512), BF16), ((27, 32, 32), BF16), ((8, 27), jnp.int32)],
        [pltpu.VMEM((8, 32, 512), BF16), send_space, vm(8, 2, 72, 128), sems(13)],
        [HBM] * 6,
        2 * 512 * 512 * 256,
        1 << 21,
    )(in_hbm(features), in_hbm(voxel_mask), send, in_hbm(grad_out), in_hbm(weights), in_hbm(kernel_map))
    first = swap(first)
    (stack,) = call(stack_kernel, [((640, 768), BF16)], [], [VMEM] * 2, 1 << 28, 2 << 20)(cot, mask)
    near, far, kmap, stack = exchange(first, own_near, own_far, kmap, stack)
    last = exchange_end(near, far)

    wide, keep_t, give_t, grad_center, xg, yg, zg, table, grad_first, grad_near, grad_far = call(
        back_kernel,
        [((768, 1024), BF16), ((384, 640), BF16), ((384, 640), BF16), center_shape]
        + face_shapes
        + [pltpu.SMEM((8, 27), jnp.int32), block(5), block(2), block(1)],
        [vm(8, 640, 128)] + accumulators + [pltpu.VMEM((8, 27), jnp.int32), sems(1)],
        [VMEM] * 3,
        2 * 640 * 768 * 1024,
        8 << 20,
    )(stack, taps_w, kmap)

    taps, give = call(
        taps_kernel,
        [((640, 1024), BF16), ((16, 896), F32)],
        accumulators,
        [VMEM] * 4 + [SMEM] + [VMEM] * 5,
    )(center, xf, yf, zf, pltpu.with_memory_space_constraint(table, pltpu.SMEM), give_t, first, near, far, last)

    (conv,) = call(
        conv_kernel, [((8, 32, 512), BF16)], [], [VMEM] * 3
    )(taps, wide, mask)

    grad_first = swap(grad_first)
    grad_near, grad_far = exchange(grad_first, grad_near, grad_far)

    (keep,) = call(keep_kernel, [((16, 896), F32)], [], [VMEM] * 2)(taps, keep_t)
    part = keep + swap(give)
    other = swap(part, 2)
    other, conv, grad_near, grad_far = lax.optimization_barrier((other, conv, grad_near, grad_far))
    part = part + other
    grad_last = exchange_end(grad_near, grad_far)
    (grad_features,) = call(
        fold_kernel,
        [((8, 32, 512), F32)],
        [vm(8, 16, 256), vm(8, 16, 256), vm(8, 64, 128), send_space, sems(1)],
        [VMEM] * 5 + [HBM] + [VMEM] * 4,
    )(grad_center, xg, yg, zg, mask, send, grad_first, grad_near, grad_far, grad_last)

    bit = 4
    while bit < lax.axis_size(RANGE_AXES):
        other = swap(part, bit)
        if bit == 8:
            other, grad_features = lax.optimization_barrier((other, grad_features))
        part = part + other
        bit *= 2
    rest = swap(part)

    brick_count, _, voxels = features.shape
    scale = 1.0 / math.sqrt(brick_count * lax.axis_size(RANGE_AXES) * voxels)
    (grad_weights,) = call(functools.partial(spread_kernel, scale), [((27, 32, 32), F32)], [], [VMEM] * 2)(part, rest)
    return conv, grad_features, grad_weights


def solution(mesh):
    bricks = ("scene", "curve", "slab")
    return jax.shard_map(
        body,
        mesh=mesh,
        in_specs=(
            P(bricks, None, None),
            P(bricks, None),
            P(),
            P(bricks, None, None),
            P(bricks, None, None),
            P(bricks, None),
        ),
        out_specs=(
            P(bricks, None, None),
            P(bricks, None, None),
            P("scene", None, None),
        ),
        check_vma=False,
    )
```

```python
import functools
import math

import jax
import jax.numpy as jnp
from jax import lax
from jax.experimental import pallas as pl
from jax.experimental.pallas import tpu as pltpu
from jax.sharding import PartitionSpec as P

F32 = jnp.float32
BF16 = jnp.bfloat16
RANGE_AXES = ("curve", "slab")
VMEM = pl.BlockSpec(memory_space=pltpu.VMEM)
HBM = pl.BlockSpec(memory_space=pltpu.HBM)
SMEM = pl.BlockSpec(memory_space=pltpu.SMEM)
NT = (((1,), (1,)), ((), ()))
NN = (((1,), (0,)), ((), ()))
TN = (((0,), (0,)), ((), ()))

BLOCK = 160
DUMMY = 24


def iota(shape, axis):
    return lax.broadcasted_iota(jnp.int32, shape, axis)


def dot(a, b, dims):
    return lax.dot_general(a, b, dims, preferred_element_type=F32)


def col(jx, jy, jz):
    return 9 * (jx + 1) + 3 * (jy + 1) + (jz + 1)


def voxel_order():
    row = iota((512, 512), 0)
    return jnp.where(iota((512, 512), 1) == ((row & 63) << 3) + (row >> 6), 1.0, 0.0).astype(BF16)


def swap_blocks(parts):
    lane = iota((64, 128), 1)
    half = [[p[:, :128], p[:, 128:]] for p in parts]
    now = [[half[(h << 2) | (i & 3)][i >> 2] for h in range(2)] for i in range(8)]
    for bit, shift in ((1, 64), (0, 32)):
        low = (lane & shift) == 0
        for i in range(8):
            if i >> bit & 1:
                continue
            j = i | (1 << bit)
            for h in range(2):
                p, q = now[i][h], now[j][h]
                now[i][h] = jnp.where(low, p, pltpu.roll(q, shift, 1))
                now[j][h] = jnp.where(low, pltpu.roll(p, 128 - shift, 1), q)
    return [jnp.concatenate(n, axis=1) for n in now]


def to_rows(values, order):
    swapped = dot(order, values, NT)
    return swap_blocks([swapped[64 * z : 64 * z + 64] for z in range(8)])


def masked_values(values, mask):
    return (values.astype(F32) * mask.astype(F32)[:, None, :]).astype(BF16).reshape(256, 512)


def parity():
    return (lax.axis_index("curve") * lax.axis_size("slab") + lax.axis_index("slab")) & 1


def fetch(*pairs):
    copies = [pltpu.make_async_copy(src, dst, sem) for src, dst, sem in pairs]
    for c in copies:
        c.start()
    return copies


def z_planes(lo, hi):
    lane = iota(lo.shape, 1)
    even = jnp.where(lane < 64, pltpu.roll(hi, 32, 1), pltpu.roll(hi, 96, 1))
    odd = jnp.where(lane < 64, pltpu.roll(lo, 32, 1), pltpu.roll(lo, 96, 1))
    return jnp.where((lane & 32) == 0, even, odd)


def half(h):
    return slice(128 * h, 128 * h + 128)


def put_block(out, at, x, y, z):
    for k in range(2):
        for h in range(2):
            row = 32 * k + 16 * h
            out[at, row : row + 16] = x[k][:, half(h)].astype(BF16)
    pieces = [y[k][a : a + 6, half(h)] for k in range(2) for h in range(2) for a in (1, 9)]
    out[at, 64:112] = jnp.concatenate(pieces, axis=0).astype(BF16)
    out[at, 112:160] = z.astype(BF16)


def get_block(ref, at):
    x = [[ref[at, 32 * k + 16 * h : 32 * k + 16 * h + 16].astype(F32) for h in range(2)] for k in range(2)]
    y = ref[at, 64:112].astype(F32)
    y = [[[y[24 * k + 12 * h + 6 * a :][:6] for a in range(2)] for h in range(2)] for k in range(2)]
    return x, y, ref[at, 112:160].astype(F32)


def pack_kernel(
    feat_hbm, mask_hbm, send_hbm, cot_hbm, weights_hbm, kmap_hbm,
    first, own_near, own_far, center, xf, yf, zf, mask, cot, weights, kmap,
    feat, send, padded, sems,
):
    bricks = [(feat_hbm.at[pl.ds(b, 1)], feat.at[pl.ds(b, 1)], sems.at[5 + b]) for b in range(8)]
    copies = fetch(*bricks, (mask_hbm, mask, sems.at[0]), (send_hbm, send, sems.at[1]))
    later = fetch((cot_hbm, cot, sems.at[2]), (weights_hbm, weights, sems.at[3]), (kmap_hbm, kmap, sems.at[4]))
    order = voxel_order()
    for c in copies:
        c.wait()
    bricks = to_rows(masked_values(feat[...], mask[...]), order)
    lane = iota((48, 128), 1)
    for b in range(8):
        c = bricks[b]
        for h in range(2):
            center[b, h] = c[:, 128 * h : 128 * h + 128]
            padded[b, h, 0:64] = c[:, 128 * h : 128 * h + 128]
        xf[b, 0:8] = c[0:8]
        xf[b, 8:16] = c[56:64]
        for h in range(2):
            s = slice(128 * h, 128 * h + 128)
            yf[b, 0:8, s] = padded[b, h, pl.ds(0, 8, 8), :]
            yf[b, 8:16, s] = padded[b, h, pl.ds(7, 8, 8), :]
        zf[b] = z_planes(c[:, :128], c[:, 128:])
    flip = parity() * 4

    def put(out, at, u):
        pick = [jnp.maximum(send[k, u], 0) for k in range(2)]
        z = jnp.where(lane < 64, zf[pick[0], 8:56], zf[pick[1], 8:56])
        put_block(out, at, [xf[p] for p in pick], [yf[p] for p in pick], z)

    for n in range(4):
        put(first, n, (4 + n) ^ flip)
    put(first, 4, flip)
    for n in range(2):
        put(own_near, n, (1 + n) ^ flip)
    put(own_far, 0, 3 ^ flip)
    for c in later:
        c.wait()


def sublane_masks(rows):
    y = iota((rows, 8, 128), 1)
    return y == 0, y == 7


def stack_kernel(cot, mask, weights, stack, wide):
    order = voxel_order()
    bricks = to_rows(masked_values(cot[...], mask[...]), order)
    for b in range(8):
        c = bricks[b]
        for d in range(3):
            before, after = jnp.zeros((8 * d, 256), F32), jnp.zeros((16 - 8 * d, 256), F32)
            pieces = [p for p in (before, c, after) if p.shape[0]]
            stack[80 * b : 80 * b + 80, 256 * d : 256 * d + 256] = jnp.concatenate(pieces, axis=0).astype(BF16)

    tile = jnp.where((iota((32, 256), 1) & 31) == iota((32, 256), 0), 1.0, 0.0).astype(BF16)
    tiled = dot(weights[...].reshape(864, 32), tile, NN)
    block = iota((32, 256), 1) >> 5

    def tap(dx, dy, dz):
        t = col(dx - 1, dy - 1, dz - 1)
        return tiled[32 * t : 32 * t + 32]

    for dx in range(3):
        for z in range(8):
            rows = slice(256 * dx + 32 * z, 256 * dx + 32 * z + 32)
            for dy in range(3):
                w = jnp.zeros((32, 256), F32)
                for dz in range(3):
                    if 0 <= z + dz - 1 <= 7:
                        w = jnp.where(block == z + dz - 1, tap(dx, dy, dz), w)
                wide[rows, 256 * dy : 256 * dy + 256] = w.astype(BF16)
            w = jnp.zeros((32, 256), F32)
            if z in (0, 7):
                for dy in range(3):
                    w = jnp.where(block == 2 * dy + (z == 7), tap(dx, dy, 0 if z == 0 else 2), w)
            wide[rows, 768:1024] = w.astype(BF16)


def back_kernel(
    stack, wide, kmap,
    keep_t, give_t, center, xg, yg, zg, table, first, own_near, own_far,
    gp, xa, ya, za, entries, sem,
):
    e = kmap[...]
    entries[...] = jnp.where(e < 0, DUMMY, jnp.where(e < 8, e, ((e - 8) ^ (parity() * 8)) + 8))
    to_table = fetch((entries, table, sem.at[0]))[0]
    odd = parity() == 1
    for d in range(3):
        turned = stack[:, 256 * d : 256 * d + 256].T.reshape(8, 2, 16, 640)
        top, bottom = turned[:, 0].reshape(128, 640), turned[:, 1].reshape(128, 640)
        keep_t[128 * d : 128 * d + 128] = jnp.where(odd, bottom, top)
        give_t[128 * d : 128 * d + 128] = jnp.where(odd, top, bottom)

    for n in range(4):
        s = slice(256 * n, 256 * n + 256)
        g = dot(stack[...], wide[:, s], NN)
        gp[2 * n] = g[:, :128]
        gp[2 * n + 1] = g[:, 128:]

    xa[...] = jnp.zeros_like(xa)
    ya[...] = jnp.zeros_like(ya)
    za[...] = jnp.zeros_like(za)
    to_table.wait()
    low3 = iota((10, 8, 128), 2) < 32

    def brick(b, carry):
        base = pl.multiple_of(80 * b, 80)
        e = lambda *j: table[b, col(*j)]
        y0, y7 = sublane_masks(10)
        for h in range(2):
            s = slice(128 * h, 128 * h + 128)

            def part(n):
                return gp[2 * n + h, pl.ds(base, 80)].reshape(10, 8, 128)

            below, above = part(0), part(2)
            r = (
                part(1)
                + jnp.where(y7, 0.0, pltpu.roll(below, 7, 1))
                + jnp.where(y0, 0.0, pltpu.roll(above, 1, 1))
            )
            center[b, h] = r[1:9].reshape(64, 128)
            xa[e(-1, 0, 0), 8:16, s] += r[0]
            xa[e(1, 0, 0), 0:8, s] += r[9]
            ya[e(0, -1, 0), 8:16, s] += gp[h, pl.ds(base + 8, 8, 8), :]
            ya[e(0, 1, 0), 0:8, s] += gp[4 + h, pl.ds(base + 15, 8, 8), :]
            xa[e(-1, -1, 0), 15:16, s] += below[0, 0:1]
            xa[e(1, -1, 0), 7:8, s] += below[9, 0:1]
            xa[e(-1, 1, 0), 8:9, s] += above[0, 7:8]
            xa[e(1, 1, 0), 0:1, s] += above[9, 7:8]
        a = gp[6, pl.ds(base, 80)].reshape(10, 8, 128)
        below = pltpu.roll(a, 7, 1)
        above = pltpu.roll(gp[7, pl.ds(base, 80)].reshape(10, 8, 128), 1, 1)
        r = pltpu.roll(a, 64, 2) + jnp.where(y7, 0.0, below) + jnp.where(y0, 0.0, above)
        below = jnp.where(y7, below, 0.0)
        above = jnp.where(y0, above, 0.0)
        for jy, v in ((0, r), (-1, below), (1, above)):
            for jz in (-1, 1):
                w = jnp.where(low3 if jz < 0 else ~low3, v, 0.0)
                za[e(0, jy, jz)] += w[1:9].reshape(64, 128)
                za[e(-1, jy, jz), 56:64] += w[0]
                za[e(1, jy, jz), 0:8] += w[9]
        return carry

    lax.fori_loop(0, 8, brick, 0, unroll=2)
    for i in range(8):
        xg[i] = xa[i]
        yg[i] = ya[i]
        zg[i] = za[i]

    lane = iota((48, 128), 1)
    edge_lane = iota((16, 128), 1)

    def put(out, at, n):
        entry = 8 + 2 * (n ^ 4)
        x, y = [], []
        for e in (entry, entry + 1):
            for row, from_row in ((0, 0), (7, 8), (8, 7), (15, 15)):
                xa[e, row : row + 1] += ya[e, from_row : from_row + 1]
            z = pltpu.roll(jnp.concatenate([za[e, 0:8], za[e, 56:64]], axis=0), 96, 1)
            lo = xa[e, :, :128] + jnp.where(edge_lane < 32, z, 0.0)
            hi = xa[e, :, 128:] + jnp.where(edge_lane >= 96, z, 0.0)
            x.append(jnp.concatenate([lo, hi], axis=1))
            y.append(ya[e])
        z = jnp.where(lane < 64, za[entry, 8:56], pltpu.roll(za[entry + 1, 8:56], 64, 1))
        put_block(out, at, x, y, z)

    for n in range(4):
        put(first, n, 4 + n)
    put(first, 4, 0)
    for n in range(2):
        put(own_near, n, 1 + n)
    put(own_far, 0, 3)


def received(first, near, far, last):
    return [(last, 1), (last, 0), (far, 1), (far, 0), (first, 4), (near, 3), (near, 1), (last, 2)]


def band_product(half_t, taps):
    product = dot(half_t, taps, NN)
    lane = iota((16, 128), 1)
    tiles = [jnp.zeros((16, 128), F32) for _ in range(7)]
    for n in range(9):
        dx, dy = n // 3, n % 3
        total = jnp.zeros((16, 128), F32)
        for z in range(8):
            rows = product[128 * dx + 16 * z : 128 * dx + 16 * z + 16]
            lo = rows[:, 256 * dy : 256 * dy + 128]
            hi = rows[:, 256 * dy + 128 : 256 * dy + 256]
            edge = rows[:, 768 + 128 * (dy // 2) : 896 + 128 * (dy // 2)]
            at = 64 * (dy % 2)
            if z == 0:
                v = jnp.where(lane < 32, pltpu.roll(edge, (128 - at) % 128, 1), pltpu.roll(lo, 32, 1))
            elif z == 7:
                v = jnp.where(lane < 64, pltpu.roll(hi, 64, 1), pltpu.roll(edge, (32 - at) % 128, 1))
            else:
                q = 32 * (z - 1)
                left, right = (lo, lo) if q < 64 else (lo, hi) if q < 128 else (hi, hi)
                if left is right:
                    v = pltpu.roll(left, (256 - q) % 128, 1) if q % 128 else left
                else:
                    v = jnp.where(lane < 128 - q, pltpu.roll(left, 128 - q, 1), pltpu.roll(right, 128 - q, 1))
            total = total + v
        piece = jnp.where(lane < 96, total, 0.0)
        at, tile = 96 * n % 128, 96 * n // 128
        turned = pltpu.roll(piece, at, 1) if at else piece
        if at + 96 <= 128:
            tiles[tile] = tiles[tile] + turned
        else:
            tiles[tile] = tiles[tile] + jnp.where(lane >= at, turned, 0.0)
            tiles[tile + 1] = tiles[tile + 1] + jnp.where(lane < at, turned, 0.0)
    return jnp.concatenate(tiles, axis=1)


def taps_kernel(
    center, xf, yf, zf, table, give_t, first, near, far, last, taps, give, xt, yt, zt
):
    for i in range(8):
        xt[i] = xf[i]
        yt[i] = yf[i]
        zt[i] = zf[i]
    xt[DUMMY] = jnp.zeros((16, 256), F32)
    yt[DUMMY] = jnp.zeros((16, 256), F32)
    zt[DUMMY] = jnp.zeros((64, 128), F32)
    lane = iota((48, 128), 1)
    for n, (ref, at) in enumerate(received(first, near, far, last)):
        x, y, z = get_block(ref, at)
        for k in range(2):
            entry = 8 + 2 * n + k
            for h in range(2):
                plane = x[k][h]
                xt[entry, :, half(h)] = plane
                yt[entry, 1:7, half(h)] = y[k][h][0]
                yt[entry, 9:15, half(h)] = y[k][h][1]
                for row, from_row in ((0, 0), (8, 7), (7, 8), (15, 15)):
                    yt[entry, row : row + 1, half(h)] = plane[from_row : from_row + 1]
            edges = z_planes(x[k][0], x[k][1])
            zt[entry, 0:8] = edges[0:8]
            zt[entry, 56:64] = edges[8:16]
        turned = pltpu.roll(z, 64, 1)
        zt[8 + 2 * n, 8:56] = jnp.where(lane < 64, z, turned)
        zt[9 + 2 * n, 8:56] = jnp.where(lane < 64, turned, z)

    low3 = (iota((8, 8, 128), 2) & 32) == 0
    low2 = (iota((8, 128), 1) & 32) == 0
    left3 = iota((10, 8, 128), 2) < 64

    def brick(b, carry):
        base = pl.multiple_of(80 * b, 16)
        e = lambda *j: table[b, col(*j)]
        y0, y7 = sublane_masks(10)
        for h in range(2):
            s = slice(128 * h, 128 * h + 128)
            r = jnp.concatenate(
                [
                    xt[e(-1, 0, 0), 8:16, s].reshape(1, 8, 128),
                    center[b, h].reshape(8, 8, 128),
                    xt[e(1, 0, 0), 0:8, s].reshape(1, 8, 128),
                ],
                axis=0,
            )

            def edge(jy, y_rows, x_row):
                first_row = xt[e(-1, jy, 0), 8 + x_row : 9 + x_row, s]
                last_row = xt[e(1, jy, 0), x_row : x_row + 1, s]
                entry = e(0, jy, 0)
                middle = [yt[entry, y_rows + x : y_rows + x + 1, s] for x in range(8)]
                rows = [first_row] + middle + [last_row]
                return jnp.stack([jnp.broadcast_to(row, (8, 128)) for row in rows], axis=0)

            below = jnp.where(y0, edge(-1, 8, 7), pltpu.roll(r, 1, 1))
            above = jnp.where(y7, edge(1, 0, 0), pltpu.roll(r, 7, 1))
            for n, v in enumerate((below, r, above)):
                taps[pl.ds(base, 80), 256 * n + 128 * h : 256 * n + 128 * h + 128] = v.reshape(80, 128).astype(BF16)

        def halo(jy):
            lo, hi = e(0, jy, -1), e(0, jy, 1)
            middle = jnp.where(low3, zt[lo].reshape(8, 8, 128), zt[hi].reshape(8, 8, 128))
            start = jnp.where(low2, zt[e(-1, jy, -1), 56:64], zt[e(-1, jy, 1), 56:64])
            end = jnp.where(low2, zt[e(1, jy, -1), 0:8], zt[e(1, jy, 1), 0:8])
            return jnp.concatenate([start[None], middle, end[None]], axis=0)

        r = halo(0)
        below = pltpu.roll(jnp.where(y7, halo(-1), r), 1, 1)
        above = pltpu.roll(jnp.where(y0, halo(1), r), 7, 1)
        taps[pl.ds(base, 80), 768:896] = jnp.where(left3, below, r).reshape(80, 128).astype(BF16)
        taps[pl.ds(base, 80), 896:1024] = jnp.where(left3, above, 0.0).reshape(80, 128).astype(BF16)
        return carry

    lax.fori_loop(0, 8, brick, 0, unroll=8)

    give[...] = band_product(give_t[...], taps[...])


def keep_kernel(taps, keep_t, keep):
    keep[...] = band_product(keep_t[...], taps[...])


def conv_kernel(taps, wide, mask, conv):
    pre = jnp.zeros((8, 8, 8, 256), F32)
    for dx in range(3):
        u = dot(taps[...], wide[256 * dx : 256 * dx + 256], NT).reshape(8, 10, 8, 256)
        pre = pre + u[:, dx : dx + 8]
    by_z = swap_blocks([pre[b].reshape(64, 256) for b in range(8)])
    stacked = jnp.concatenate([v.astype(BF16) for v in by_z], axis=0)
    out = dot(stacked.T, voxel_order(), NN).reshape(8, 32, 512)
    conv[...] = (out * mask[...].astype(F32)[:, None, :]).astype(BF16)


def fold_kernel(center, xg, yg, zg, mask, send_hbm, first, near, far, last, out, xa, ya, za, send, sem):
    to_send = fetch((send_hbm, send, sem.at[0]))[0]
    flip = parity() * 4
    xa[...] = xg[...]
    ya[...] = yg[...]
    za[...] = zg[...]
    to_send.wait()
    for n, (ref, at) in enumerate(received(first, near, far, last)):
        u = n ^ 4 ^ flip
        x, y, z = get_block(ref, at)
        for k in range(2):
            i = jnp.maximum(send[k, u], 0)
            for h in range(2):
                xa[i, :, half(h)] += x[k][h]
                ya[i, 1:7, half(h)] += y[k][h][0]
                ya[i, 9:15, half(h)] += y[k][h][1]
            za[i, 8:56] += pltpu.roll(z, 64, 1) if k else z
    y0, y7 = sublane_masks(8)
    lane = iota((64, 128), 1)
    bricks = []
    for b in range(8):
        turned = pltpu.roll(za[b], 96, 1)
        halves = []
        for h in range(2):
            s = slice(128 * h, 128 * h + 128)
            c = center[b, h] + jnp.where(lane >= 96 if h else lane < 32, turned, 0.0)
            c = c.reshape(8, 8, 128)
            c = jnp.concatenate([c[0:1] + xa[b, 0:8, s][None], c[1:7], c[7:8] + xa[b, 8:16, s][None]], axis=0)
            low = jnp.stack([jnp.broadcast_to(ya[b, x : x + 1, s], (8, 128)) for x in range(8)], axis=0)
            high = jnp.stack([jnp.broadcast_to(ya[b, 8 + x : 9 + x, s], (8, 128)) for x in range(8)], axis=0)
            c = c + jnp.where(y0, low, 0.0) + jnp.where(y7, high, 0.0)
            halves.append(c.reshape(64, 128))
        bricks.append(jnp.concatenate(halves, axis=1))
    rows = jnp.concatenate(swap_blocks(bricks), axis=0).T
    coarse = rows.astype(BF16)
    fine = (rows - coarse.astype(F32)).astype(BF16)
    order = voxel_order()
    full = dot(coarse, order, NN) + dot(fine, order, NN)
    out[...] = full.reshape(8, 32, 512) * mask[...].astype(F32)[:, None, :]


def spread_kernel(scale, mine, other, out):
    odd = parity() == 1
    a, b = mine[...], other[...]
    wide = jnp.concatenate([jnp.where(odd, b, a), jnp.where(odd, a, b)], axis=0) * scale
    for t in range(27):
        at, tile = 32 * t % 128, 32 * t // 128
        v = wide[:, 128 * tile : 128 * tile + 128]
        v = pltpu.roll(v, 128 - at, 1) if at else v
        out[t] = v[:, :32]


def call(kernel, outs, scratch, ins, flops=0, size=0):
    return pl.pallas_call(
        kernel,
        out_shape=[jax.ShapeDtypeStruct(*o) if isinstance(o, tuple) else o for o in outs],
        in_specs=ins,
        out_specs=[VMEM if isinstance(o, tuple) else SMEM for o in outs],
        scratch_shapes=scratch,
        compiler_params=pltpu.CompilerParams(vmem_limit_bytes=40 * 1024 * 1024),
        cost_estimate=pl.CostEstimate(flops=flops, bytes_accessed=size, transcendentals=0),
    )


def permute(value, target):
    count = lax.axis_size(RANGE_AXES)
    return lax.ppermute(value, RANGE_AXES, [(r, target(r, count)) for r in range(count)])


def in_hbm(value):
    return pltpu.with_memory_space_constraint(value, pltpu.HBM)


def swap(value, bit=1):
    return permute(value, lambda r, count: r ^ bit)


def onward(value, pairs, cross):
    return permute(value, lambda r, count: ((r + (-2 * pairs if r & 1 else 2 * pairs)) % count) ^ cross)


def exchange(first, near, far, *later):
    near = jnp.concatenate([near, first[0:2]], axis=0)
    far = jnp.concatenate([far, first[2:4]], axis=0)
    near, far, *later = lax.optimization_barrier((near, far, *later))
    near = onward(near, 1, 1)
    return near, onward(far, 2, 0), *later


def exchange_end(near, far):
    return swap(jnp.concatenate([near[0:1], near[2:3], far[2:3]], axis=0))


def body(features, voxel_mask, weights, grad_out, send_list, kernel_map):
    block = lambda n: ((n, BLOCK, 128), BF16)
    vm = lambda *shape: pltpu.VMEM(shape, F32)
    center_shape = ((8, 2, 64, 128), F32)
    face_shapes = [((8, 16, 256), F32), ((8, 16, 256), F32), ((8, 64, 128), F32)]
    accumulators = [vm(25, 16, 256), vm(25, 16, 256), vm(25, 64, 128)]
    send_space = pltpu.SMEM((2, 8), jnp.int32)
    sems = lambda n: pltpu.SemaphoreType.DMA((n,))
    send = in_hbm(send_list[0].T)

    first, own_near, own_far, center, xf, yf, zf, mask, cot, taps_w, kmap = call(
        pack_kernel,
        [block(5), block(2), block(1), center_shape]
        + face_shapes
        + [((8, 512), jnp.int32), ((8, 32, 512), BF16), ((27, 32, 32), BF16), ((8, 27), jnp.int32)],
        [pltpu.VMEM((8, 32, 512), BF16), send_space, vm(8, 2, 72, 128), sems(13)],
        [HBM] * 6,
        2 * 512 * 512 * 256,
        1 << 21,
    )(in_hbm(features), in_hbm(voxel_mask), send, in_hbm(grad_out), in_hbm(weights), in_hbm(kernel_map))
    first = swap(first)
    stack, wide = call(
        stack_kernel, [((640, 768), BF16), ((768, 1024), BF16)], [], [VMEM] * 3, 1 << 28, 2 << 20
    )(cot, mask, taps_w)
    near, far, kmap, stack, wide = exchange(first, own_near, own_far, kmap, stack, wide)
    last = exchange_end(near, far)

    keep_t, give_t, grad_center, xg, yg, zg, table, grad_first, grad_near, grad_far = call(
        back_kernel,
        [((384, 640), BF16), ((384, 640), BF16), center_shape]
        + face_shapes
        + [pltpu.SMEM((8, 27), jnp.int32), block(5), block(2), block(1)],
        [vm(8, 640, 128)] + accumulators + [pltpu.VMEM((8, 27), jnp.int32), sems(1)],
        [VMEM] * 3,
        2 * 640 * 768 * 1024,
        8 << 20,
    )(stack, wide, kmap)

    taps, give = call(
        taps_kernel,
        [((640, 1024), BF16), ((16, 896), F32)],
        accumulators,
        [VMEM] * 4 + [SMEM] + [VMEM] * 5,
    )(center, xf, yf, zf, pltpu.with_memory_space_constraint(table, pltpu.SMEM), give_t, first, near, far, last)

    (conv,) = call(
        conv_kernel, [((8, 32, 512), BF16)], [], [VMEM] * 3
    )(taps, wide, mask)

    grad_first = swap(grad_first)
    grad_near, grad_far = exchange(grad_first, grad_near, grad_far)

    (keep,) = call(keep_kernel, [((16, 896), F32)], [], [VMEM] * 2)(taps, keep_t)
    part = keep + swap(give)
    other = swap(part, 2)
    other, conv, grad_near, grad_far = lax.optimization_barrier((other, conv, grad_near, grad_far))
    part = part + other
    grad_last = exchange_end(grad_near, grad_far)
    (grad_features,) = call(
        fold_kernel,
        [((8, 32, 512), F32)],
        [vm(8, 16, 256), vm(8, 16, 256), vm(8, 64, 128), send_space, sems(1)],
        [VMEM] * 5 + [HBM] + [VMEM] * 4,
    )(grad_center, xg, yg, zg, mask, send, grad_first, grad_near, grad_far, grad_last)

    bit = 4
    while bit < lax.axis_size(RANGE_AXES):
        other = swap(part, bit)
        if bit == 8:
            other, grad_features = lax.optimization_barrier((other, grad_features))
        part = part + other
        bit *= 2
    rest = swap(part)

    brick_count, _, voxels = features.shape
    scale = 1.0 / math.sqrt(brick_count * lax.axis_size(RANGE_AXES) * voxels)
    (grad_weights,) = call(functools.partial(spread_kernel, scale), [((27, 32, 32), F32)], [], [VMEM] * 2)(part, rest)
    return conv, grad_features, grad_weights


def solution(mesh):
    bricks = ("scene", "curve", "slab")
    return jax.shard_map(
        body,
        mesh=mesh,
        in_specs=(
            P(bricks, None, None),
            P(bricks, None),
            P(),
            P(bricks, None, None),
            P(bricks, None, None),
            P(bricks, None),
        ),
        out_specs=(
            P(bricks, None, None),
            P(bricks, None, None),
            P("scene", None, None),
        ),
        check_vma=False,
    )
```
